1024 devices in a mesh: dp: 32 (over z), node: 8 (over y, core), local: 4 (over x).
Axes of the slice: x: 4, y: 4, z: 32, core: 2. Of those that a mesh axis runs over, the one named last changes fastest.
Arguments:
- tokens: bfloat16 [1024, 7168], P(('dp', 'local')), may hold values from -6 to 6
- out_grad: bfloat16 [1024, 7168], P(('dp', 'local')), may hold values from -1.1953125 to 1.1953125
- picks: int32 [1024, 8], P(('dp', 'local')), may hold values from 0 to 31, all different within a row; in each aligned block of 8 rows (0 to 7, 8 to 15, ...) at most 4 rows name the same one
- gates: bfloat16 [1024, 8], P(('dp', 'local')), may hold values from 0.099609375 to 1
- w_gate: bfloat16 [32, 7168, 1024], P('dp', None, 'node'), may hold values from -0.0625 to 0.0625
- w_up: bfloat16 [32, 7168, 1024], P('dp', None, 'node'), may hold values from -0.0625 to 0.0625
- w_down: bfloat16 [32, 1024, 7168], P('dp', 'node'), may hold values from -0.1875 to 0.1875
Outputs:
- in_grad: bfloat16 [1024, 7168], P(('dp', 'local'), 'node')
- gate_grad: float32 [1024, 8], P(('dp', 'local'))
- grad_gate_w: bfloat16 [32, 7168, 1024], P('dp', 'local', 'node')
- grad_up_w: bfloat16 [32, 7168, 1024], P('dp', 'local', 'node')
- grad_down_w: bfloat16 [32, 1024, 7168], P('dp', 'node', 'local')
The draws below stay inside these ranges and needn't reach their ends.
Inputs may be any that keep to these rules, and one draw needn't show every extreme that they name: Each row names 8 different experts. Among the picks of one device's 8 tokens no expert is named more than 4 times; some expert is named exactly 4 times.
All inputs are finite; a program needn't handle non-finite values.
Results may differ from the reference program's by a relative error of at most 0.0059.
Values may be sent and summed in bfloat16 or wider, within the bound.
A program may use at most 64 MiB of HBM per device.

```python
import math
import jax
import jax.numpy as jnp
import numpy as np
from jax import lax

D = 7168
FFW = 1024
TOK_DEV = 8
EXPERTS = 32
TOP = 8
CAP = 4
TOKENS = 1024


def level_of(stream_key, dims, pieces, low, largest):
    loudness = 1.0
    for axis_at, blocks in pieces:
        heights = jax.random.uniform(jax.random.fold_in(jax.random.fold_in(stream_key, 6), axis_at), (blocks,), jnp.float32, low / len(pieces), largest / len(pieces))
        loudness = loudness * jnp.repeat(jnp.exp(heights), dims[axis_at] // blocks).reshape((-1,) + (1,) * (len(dims) - 1 - axis_at))
    return loudness


def assign_block(own_key, own, number, rows, amount, top, limit, skew):
    sequence = jax.random.permutation(own_key, amount)
    heavy_load, common = load_shares(amount, rows * top, limit, skew, True), load_shares(amount, rows * top, limit, skew, False)
    places = jnp.arange(amount)

    def named(tallies, rotation):
        used = int((tallies > 0).sum())
        fixed = max(1, used // 4)
        moved = fixed + (places - fixed + rotation * (used - fixed)) % max(1, amount - fixed)
        return jnp.zeros((amount,), jnp.int32).at[sequence[jnp.where(places < fixed, places, moved)]].set(jnp.asarray(tallies, jnp.int32))

    tallies = jnp.where(number % 4 == 0, named(heavy_load, number // 4), named(common, number - number // 4 - 1))
    mixed = jax.random.permutation(jax.random.fold_in(own, 3), amount)
    source_of, taker = mixed[0:amount // 2 * 2:2], mixed[1:amount // 2 * 2:2]
    margin = jnp.minimum(tallies[source_of] - 1, limit - tallies[taker]) // 2
    margin = jnp.where((source_of == sequence[0]) | (taker == sequence[0]) | (tallies[taker] == 0), 0, jnp.maximum(margin, 0))
    moved = jax.random.randint(jax.random.fold_in(own, 4), (amount // 2,), 0, 1 << 20) % (margin + 1)
    tallies = tallies.at[source_of].add(-moved).at[taker].add(moved)
    labels = jnp.searchsorted(jnp.cumsum(tallies), jnp.arange(rows * top), side="right").astype(jnp.int32)
    listing = labels.reshape(top, rows).T
    listing = listing[jax.random.permutation(jax.random.fold_in(own, 1), rows)]
    rotation = jax.random.randint(jax.random.fold_in(own, 2), (rows, 1), 0, top)
    return jnp.take_along_axis(listing, (jnp.arange(top)[None, :] + rotation) % top, axis=1)


def load_shares(amount, total, limit, slope, full):
    portions = [(1 << 20) // math.isqrt(standing ** slope) + 1 for standing in range(1, amount + 1)]
    largest = limit if full else min(limit, max(-(-total // amount), total * portions[0] // sum(portions)))
    least = 1 if total - largest >= amount - 1 else 0
    given, spare = [largest] + [least] * (amount - 1), total - largest - least * (amount - 1)
    while spare > 0:
        candidates = [i for i in range(1, amount) if given[i] < largest] or [i for i in range(1, amount) if given[i] < limit]
        mass, left = sum([portions[i] for i in candidates]), spare
        for i in candidates:
            extra = min(limit - given[i], max(1, left * portions[i] // mass), spare)
            given[i] = given[i] + extra
            spare = spare - extra
    return np.array(given)


def noise(stream_key, dims, spread, most, shards=(), held_as=jnp.bfloat16):
    entries = spread * jax.random.normal(stream_key, dims, jnp.float32)
    if shards:
        entries = entries * level_of(stream_key, dims, shards, -0.22, 0.18)
    return jnp.clip(entries, -most, most).astype(held_as)


def setup_inputs(seed: int = 0) -> dict:
    seeds = jax.random.split(jax.random.key(seed), 8)
    tokens = noise(seeds[0], (TOKENS, D), 1.0, 6.0, ((0, 128),))
    out_grad = noise(seeds[1], (TOKENS, D), 0.2, 1.1953125, ((0, 128),))
    picks_keys = jax.random.split(jax.random.fold_in(seeds[2], 1), TOKENS // TOK_DEV)
    picks_turns = jax.random.permutation(jax.random.fold_in(seeds[2], 3), TOKENS // TOK_DEV)
    picks = jax.vmap(lambda own, number: assign_block(jax.random.fold_in(seeds[2], 2), own, number, TOK_DEV, EXPERTS, TOP, CAP, 2))(picks_keys, picks_turns).reshape((TOKENS, TOP))
    gates = jnp.clip(0.099609375 + 0.9003906 * jax.random.uniform(seeds[3], (TOKENS, TOP), jnp.float32) ** level_of(seeds[3], (TOKENS, TOP), ((0, 128),), -0.2, 0.2), 0.099609375, 1.0).astype(jnp.bfloat16)
    w_gate = noise(seeds[4], (EXPERTS, D, FFW), D ** -0.5, 0.0625, ((0, 32), (2, 8)))
    w_up = noise(seeds[5], (EXPERTS, D, FFW), D ** -0.5, 0.0625, ((0, 32), (2, 8)))
    w_down = noise(seeds[6], (EXPERTS, FFW, D), FFW ** -0.5, 0.1875, ((0, 32), (1, 8)))
    return dict(tokens=tokens, out_grad=out_grad, picks=picks, gates=gates, w_gate=w_gate, w_up=w_up, w_down=w_down)


def reference(tokens, out_grad, picks, gates, w_gate, w_up, w_down):
    blocks = TOKENS // TOK_DEV
    per_block = TOK_DEV * TOP
    flat_picks = picks.reshape(blocks, per_block)
    position = jnp.arange(per_block, dtype=jnp.int32)
    matching = flat_picks[:, :, None] == flat_picks[:, None, :]
    earlier = position[None, :] < position[:, None]
    rank_in = jnp.sum(jnp.logical_and(matching, earlier[None]), axis=2).astype(jnp.int32)
    block_ids = jnp.arange(blocks, dtype=jnp.int32)[:, None]
    column = (block_ids * CAP + rank_in).reshape(-1).astype(jnp.int32)
    token_id = (block_ids * TOK_DEV + position[None, :] // TOP).reshape(-1).astype(jnp.int32)
    pick_id = jnp.broadcast_to(position % TOP, (blocks, per_block)).reshape(-1).astype(jnp.int32)
    expert_id = picks.reshape(-1).astype(jnp.int32)
    slot_width = blocks * CAP
    token_table = jnp.zeros((EXPERTS, slot_width), jnp.int32).at[expert_id, column].set(token_id)
    pick_table = jnp.zeros((EXPERTS, slot_width), jnp.int32).at[expert_id, column].set(pick_id)
    live_table = jnp.zeros((EXPERTS, slot_width), jnp.float32).at[expert_id, column].set(1.0)

    def expert_step(carry, inputs):
        in_acc, gate_acc = carry
        gate_mat, up_mat, down_mat, token_rows, pick_rows, live_rows = inputs
        live_b = live_rows.astype(jnp.bfloat16)[:, None]
        rows_x = tokens[token_rows] * live_b
        rows_dy = out_grad[token_rows] * live_b
        gate_val = gates[token_rows, pick_rows].astype(jnp.float32) * live_rows
        gate_pre = jnp.dot(rows_x, gate_mat, preferred_element_type=jnp.float32)
        up_pre = jnp.dot(rows_x, up_mat, preferred_element_type=jnp.float32)
        sigmoid_pre = jax.nn.sigmoid(gate_pre)
        act = gate_pre * sigmoid_pre * up_pre
        act_b = act.astype(jnp.bfloat16)
        back = jnp.dot(rows_dy, down_mat.T, preferred_element_type=jnp.float32)
        gate_part = jnp.sum(back * act, axis=1)
        gate_col = gate_val[:, None]
        scaled = (gate_col * rows_dy.astype(jnp.float32)).astype(jnp.bfloat16)
        d_act = gate_col * back
        d_up = (d_act * gate_pre * sigmoid_pre).astype(jnp.bfloat16)
        d_pre = (d_act * up_pre * sigmoid_pre * (1.0 + gate_pre * (1.0 - sigmoid_pre))).astype(jnp.bfloat16)
        slot_grad = jnp.dot(d_pre, gate_mat.T, preferred_element_type=jnp.float32)
        slot_grad = slot_grad + jnp.dot(d_up, up_mat.T, preferred_element_type=jnp.float32)
        in_acc = in_acc.at[token_rows].add(slot_grad * live_rows[:, None])
        gate_acc = gate_acc.at[token_rows, pick_rows].add(gate_part * live_rows)
        grad_gate = jnp.dot(rows_x.T, d_pre, preferred_element_type=jnp.float32).astype(jnp.bfloat16)
        grad_up = jnp.dot(rows_x.T, d_up, preferred_element_type=jnp.float32).astype(jnp.bfloat16)
        grad_down = jnp.dot(act_b.T, scaled, preferred_element_type=jnp.float32).astype(jnp.bfloat16)
        return (in_acc, gate_acc), (grad_gate, grad_up, grad_down)

    start = (jnp.zeros((TOKENS, D), jnp.float32), jnp.zeros((TOKENS, TOP), jnp.float32))
    (in_acc, gate_acc), (grad_gate_w, grad_up_w, grad_down_w) = lax.scan(
        expert_step, start, (w_gate, w_up, w_down, token_table, pick_table, live_table))
    return (in_acc.astype(jnp.bfloat16), gate_acc, grad_gate_w, grad_up_w, grad_down_w)
```

```python
import functools

import jax
import jax.numpy as jnp
from jax import lax
from jax.experimental import pallas as pl
from jax.experimental.pallas import tpu as pltpu
from jax.sharding import PartitionSpec as P

F32 = jnp.float32
BF16 = jnp.bfloat16
MESH = pl.DeviceIdType.MESH
SLOTS = 128
RING = 4
LANES = 128


def dot(left, right, contract=(1, 0)):
    dims = (((contract[0],), (contract[1],)), ((), ()))
    return lax.dot_general(left, right, dims, preferred_element_type=F32)


def kernel(
    sizes,
    tok_ref,
    dy_ref,
    picks_ref,
    gates_ref,
    wg_hbm,
    wu_hbm,
    wd_hbm,
    in_grad_ref,
    gate_grad_ref,
    gg_hbm,
    gu_hbm,
    gd_hbm,
    own_chunk,
    got_chunk,
    own_meta,
    got_meta,
    ring,
    meta_tok,
    sel_tok,
    gate_slot,
    xd,
    wgu,
    wdn,
    part,
    part_in,
    hid,
    half_out,
    half_in,
    acc,
    acc_out,
    acc_in,
    gate_rows,
    dense,
    from_right,
    from_left,
    last_out,
    last_in,
    gg_buf,
    gu_buf,
    gd_buf,
    send_sem,
    recv_sem,
    zsend_sem,
    zrecv_sem,
    rsend_sem,
    rrecv_sem,
    local_sem,
):
    zs, top = sizes
    toks = 8 * zs
    half = own_chunk.shape[1]
    colw = 2 * half
    z = lax.axis_index("dp")
    n = lax.axis_index("node")
    x = lax.axis_index("local")
    y = n // 2
    c = n % 2
    zr, zl = (z + 1) % zs, (z + zs - 1) % zs
    xr, xl, xo = (x + 1) % RING, (x + 3) % RING, (x + 2) % RING
    yr, yl, yo = (y + 1) % RING, (y + 3) % RING, (y + 2) % RING
    nodes = 2 * RING
    sibling = (z, 2 * y + 1 - c, x)
    y_right, y_left = (z, 2 * yr + c, x), (z, 2 * yl + c, x)
    x_right, x_left = (z, n, xr), (z, n, xl)
    z_right, z_left = (zr, n, x), (zl, n, x)
    across = (z, 2 * x + c, y)
    moved = x != y

    count = [0]
    sends = []

    def remote(src, dst, device, keep=True):
        i = count[0]
        count[0] += 1
        copy = pltpu.make_async_remote_copy(
            src_ref=src,
            dst_ref=dst,
            send_sem=send_sem.at[i],
            recv_sem=recv_sem.at[i],
            device_id=device,
            device_id_type=MESH,
        )
        if keep:
            sends.append(copy)
        return copy

    row0 = pl.multiple_of(x * colw, LANES)
    loads = [
        pltpu.make_async_copy(
            wg_hbm.at[0, pl.ds(row0, colw), :], wgu.at[:, 0:LANES], local_sem.at[0]
        ),
        pltpu.make_async_copy(
            wu_hbm.at[0, pl.ds(row0, colw), :], wgu.at[:, LANES : 2 * LANES], local_sem.at[1]
        ),
        pltpu.make_async_copy(wd_hbm.at[0, :, pl.ds(row0, colw)], wdn, local_sem.at[2]),
    ]
    for load in loads:
        load.start()

    barrier = pltpu.get_barrier_semaphore()
    peers = [z_right, z_left]
    peers += [(z, n, (x + i) % RING) for i in range(1, RING)]
    peers += [(z, (n + i) % nodes, x) for i in range(1, nodes)]
    for peer in peers:
        pl.semaphore_signal(barrier, inc=1, device_id=peer, device_id_type=MESH)

    @pl.when(moved)
    def _():
        pl.semaphore_signal(barrier, inc=1, device_id=across, device_id_type=MESH)

    col0 = pl.multiple_of(y * colw + c * half, LANES)
    own_chunk[...] = jnp.concatenate(
        [tok_ref[:, pl.ds(col0, half)].astype(F32), dy_ref[:, pl.ds(col0, half)].astype(F32)],
        axis=0,
    ).astype(BF16)
    place = lax.broadcasted_iota(jnp.int32, (top, LANES), 0)
    lane_k = lax.broadcasted_iota(jnp.int32, (top, LANES), 1)
    put_picks = (lane_k == 32 * x + place).astype(F32).astype(BF16)
    put_gates = (lane_k == 32 * x + 8 + place).astype(F32).astype(BF16)
    meta = dot(picks_ref[...].astype(F32).astype(BF16), put_picks) + dot(gates_ref[...], put_gates)
    own_meta[...] = jnp.concatenate([meta, meta], axis=0).astype(BF16)
    got_meta[x] = own_meta[...]

    pl.semaphore_wait(barrier, len(peers) + jnp.where(moved, 1, 0))

    cross = remote(own_chunk, got_chunk, across, keep=False)

    @pl.when(moved)
    def _():
        cross.start()

    @pl.when(jnp.logical_not(moved))
    def _():
        got_chunk[...] = own_chunk[...]

    metas = [
        remote(own_meta, got_meta.at[x], (z, n, (x + i) % RING)) for i in range(1, RING)
    ]
    for copy in metas:
        copy.start()
    for copy in metas:
        copy.wait_recv()
    ring[0, :, half:] = (
        (got_meta[0].astype(F32) + got_meta[1].astype(F32))
        + (got_meta[2].astype(F32) + got_meta[3].astype(F32))
    ).astype(BF16)

    @pl.when(moved)
    def _():
        cross.wait_recv()

    ring[0, :, 0:half] = got_chunk[...]

    n_right = zs // 2
    n_left = zs - 1 - n_right

    def go_right(s):
        return pltpu.make_async_remote_copy(
            src_ref=ring.at[s],
            dst_ref=ring.at[s + 1],
            send_sem=zsend_sem.at[0, s],
            recv_sem=zrecv_sem.at[s + 1],
            device_id=z_right,
            device_id_type=MESH,
        )

    def go_left(s):
        return pltpu.make_async_remote_copy(
            src_ref=ring.at[(zs - s) % zs],
            dst_ref=ring.at[zs - 1 - s],
            send_sem=zsend_sem.at[1, s],
            recv_sem=zrecv_sem.at[zs - 1 - s],
            device_id=z_left,
            device_id_type=MESH,
        )

    go_right(0).start()
    if n_left > 0:
        go_left(0).start()

        def gather_step(s, carry):
            go_right(s - 1).wait_recv()
            go_right(s).start()
            go_left(s - 1).wait_recv()
            go_left(s).start()
            return carry

        lax.fori_loop(1, n_left, gather_step, 0)
        go_right(n_left - 1).wait_recv()
        go_right(n_left).start()
        go_left(n_left - 1).wait_recv()
    go_right(n_right - 1).wait_recv()

    meta_all = ring[:, :, half:].astype(F32)[:, 0:8, :].reshape(toks, LANES)
    meta_tok[...] = meta_all
    expert = z.astype(F32)
    t_row = lax.broadcasted_iota(jnp.int32, (toks, toks), 0)
    t_col = lax.broadcasted_iota(jnp.int32, (toks, toks), 1)
    before = jnp.logical_and(t_row // 8 == t_col // 8, t_col < t_row).astype(F32).astype(BF16)
    lane = lax.broadcasted_iota(jnp.int32, (toks, LANES), 1)
    t_of = lax.broadcasted_iota(jnp.int32, (toks, LANES), 0)

    def named(group):
        near = jnp.logical_and(lane >= 32 * group, lane < 32 * group + top)
        return jnp.logical_and(meta_all == expert, near)

    def select(group):
        chosen = jnp.sum(named(group).astype(F32), axis=1, keepdims=True)
        chosen = jnp.broadcast_to(chosen, (toks, LANES))
        rank = dot(before, chosen.astype(BF16))
        ok = jnp.logical_and(chosen > 0.5, rank == (lane % 4).astype(F32))
        return jnp.logical_and(ok, t_of // 8 == lane // 4).astype(F32)

    mine = select(y)
    cube = mine.reshape(zs, 8, SLOTS)
    blank = jnp.zeros_like(cube)
    pick_rows = jnp.concatenate(
        [jnp.concatenate([cube, blank], axis=2), jnp.concatenate([blank, cube], axis=2)], axis=1
    ).reshape(16 * zs, 2 * SLOTS)
    rows = ring[:, :, 0:half].reshape(16 * zs, half)
    picked = dot(pick_rows.astype(BF16), rows, (0, 0)).astype(BF16)
    xd[c, 0, y] = picked[0:SLOTS]
    xd[c, 1, y] = picked[SLOTS:]

    to_right = [remote(xd.at[c, p, y], xd.at[c, p, y], y_right) for p in range(2)]
    to_left = [remote(xd.at[c, p, y], xd.at[c, p, y], y_left) for p in range(2)]
    to_core = [remote(xd.at[c, p, y], xd.at[c, p, y], sibling) for p in range(2)]
    on_right = remote(xd.at[c, 0, yl], xd.at[c, 0, yl], y_right)
    on_left = remote(xd.at[c, 1, yr], xd.at[c, 1, yr], y_left)
    core_l = [remote(xd.at[c, p, yl], xd.at[c, p, yl], sibling) for p in range(2)]
    core_r = [remote(xd.at[c, p, yr], xd.at[c, p, yr], sibling) for p in range(2)]
    core_o = [remote(xd.at[c, p, yo], xd.at[c, p, yo], sibling) for p in range(2)]
    to_right[0].start()
    to_left[1].start()
    to_right[1].start()
    to_left[0].start()
    to_core[0].start()
    to_core[1].start()

    rolled = pltpu.roll(meta_all, LANES - 8, 1)
    for group in range(RING):
        chosen = select(group).astype(BF16)
        sel_tok[group] = chosen
        gate_of = jnp.sum(jnp.where(named(group), rolled, 0.0), axis=1, keepdims=True)
        gate_of = jnp.broadcast_to(gate_of, (toks, LANES)).astype(BF16)
        gate_slot[group] = dot(chosen, gate_of, (0, 0))

    to_right[0].wait_recv()
    on_right.start()
    core_l[0].start()
    to_left[1].wait_recv()
    on_left.start()
    core_r[1].start()
    to_right[1].wait_recv()
    core_l[1].start()
    to_left[0].wait_recv()
    core_r[0].start()
    on_right.wait_recv()
    core_o[0].start()
    on_left.wait_recv()
    core_o[1].start()
    for copy in to_core + core_l + core_r + core_o:
        copy.wait_recv()
    for load in loads:
        load.wait()

    n_slots = RING * SLOTS
    gate_up = dot(xd[0, 0].reshape(n_slots, half), wgu[0:half]) + dot(
        xd[1, 0].reshape(n_slots, half), wgu[half:]
    )
    back_part = dot(xd[0, 1].reshape(n_slots, half), wdn[:, 0:half], (1, 1)) + dot(
        xd[1, 1].reshape(n_slots, half), wdn[:, half:], (1, 1)
    )
    part[:, :, 0:256] = gate_up.reshape(RING, SLOTS, 256)
    part[:, :, 256:] = back_part.reshape(RING, SLOTS, LANES)

    lo, hi = slice(0, SLOTS // 2), slice(SLOTS // 2, SLOTS)

    def scatter_copies(src, into, r, l, o, right, left):
        return dict(
            a1=remote(src.at[o, lo], into.at[0, lo], right),
            b1=remote(src.at[o, hi], into.at[0, hi], left),
            a2=remote(src.at[r, hi], into.at[1, hi], right),
            b2=remote(src.at[l, lo], into.at[2, lo], left),
            a3=remote(src.at[r, lo], into.at[1, lo], right),
            b3=remote(src.at[l, hi], into.at[2, hi], left),
        )

    px = scatter_copies(part, part_in, xr, xl, xo, x_right, x_left)
    px["a1"].start()
    px["b1"].start()
    px["a2"].start()
    px["b2"].start()
    px["a1"].wait_recv()
    part[xr, lo] = part[xr, lo] + part_in[0, lo]
    px["a3"].start()
    px["b1"].wait_recv()
    part[xl, hi] = part[xl, hi] + part_in[0, hi]
    px["b3"].start()
    for name in ("a2", "b2", "a3", "b3"):
        px[name].wait_recv()
    summed = part[x] + part_in[1] + part_in[2]

    gate_pre = summed[:, 0:128]
    up_pre = summed[:, 128:256]
    back = summed[:, 256:384]
    gate_col = gate_slot[x]
    sig = jax.nn.sigmoid(gate_pre)
    act = gate_pre * sig * up_pre
    d_act = gate_col * back
    d_up = d_act * gate_pre * sig
    d_pre = d_act * up_pre * sig * (1.0 + gate_pre * (1.0 - sig))
    hid[x, :, 0:128] = d_pre.astype(BF16)
    hid[x, :, 128:256] = d_up.astype(BF16)
    hid[x, :, 256:384] = act.astype(BF16)

    h_right = remote(hid.at[x], hid.at[x], x_right)
    h_left = remote(hid.at[x], hid.at[x], x_left)
    h_on_right = remote(hid.at[xl, lo], hid.at[xl, lo], x_right)
    h_on_left = remote(hid.at[xr, hi], hid.at[xr, hi], x_left)
    h_right.start()
    h_left.start()

    gate_row = jnp.sum(jnp.transpose(back * act), axis=0, keepdims=True)
    gate_rows[n] = jnp.broadcast_to(gate_row, (8, SLOTS))
    rows_out = [
        remote(gate_rows.at[n], gate_rows.at[n], (z, (n + i) % nodes, x)) for i in range(1, nodes)
    ]
    for copy in rows_out:
        copy.start()

    h_right.wait_recv()
    h_on_right.start()
    h_left.wait_recv()
    h_on_left.start()
    h_on_right.wait_recv()
    h_on_left.wait_recv()

    grads = hid[:, :, 0:256].reshape(n_slots, 256)
    other = pl.multiple_of((1 - c) * half, LANES)
    ours = pl.multiple_of(c * half, LANES)
    half_out[...] = dot(grads, wgu[pl.ds(other, half), :], (1, 1)).astype(BF16)
    core_half = remote(half_out, half_in, sibling)
    core_half.start()
    acc[...] = dot(grads, wgu[pl.ds(ours, half), :], (1, 1)).reshape(RING, SLOTS, half)
    core_half.wait_recv()
    arrived = half_in[...].astype(F32).reshape(RING, SLOTS, half)
    acc[...] = acc[...] + arrived

    py = scatter_copies(acc_out, acc_in, yr, yl, yo, y_right, y_left)
    acc_out[yo] = acc[yo].astype(BF16)
    py["a1"].start()
    py["b1"].start()
    acc_out[yr, hi] = acc[yr, hi].astype(BF16)
    py["a2"].start()
    acc_out[yl, lo] = acc[yl, lo].astype(BF16)
    py["b2"].start()

    for copy in rows_out:
        copy.wait_recv()
    gate_sum = gate_rows[0]
    for i in range(1, nodes):
        gate_sum = gate_sum + gate_rows[i]
    gate_tok = jnp.sum(sel_tok[x].astype(F32) * gate_sum[0:1], axis=1, keepdims=True)
    meta_x = jnp.zeros((toks, LANES), F32)
    for i in range(RING):
        turned = meta_tok[...] if i == 0 else pltpu.roll(meta_tok[...], LANES - 32 * i, 1)
        meta_x = jnp.where(x == i, turned, meta_x)
    hit = jnp.logical_and(meta_x == expert, lane < top)
    dense[:, :, half:] = jnp.where(hit, gate_tok, 0.0).reshape(zs, 8, LANES)

    py["a1"].wait_recv()
    acc_out[yr, lo] = (acc[yr, lo] + acc_in[0, lo].astype(F32)).astype(BF16)
    py["a3"].start()
    py["b1"].wait_recv()
    acc_out[yl, hi] = (acc[yl, hi] + acc_in[0, hi].astype(F32)).astype(BF16)
    py["b3"].start()
    for name in ("a2", "b2", "a3", "b3"):
        py[name].wait_recv()
    total = acc[y] + acc_in[1].astype(F32) + acc_in[2].astype(F32)

    sel = sel_tok[y]
    first = total.astype(BF16)
    rest = total - first.astype(F32)
    second = rest.astype(BF16)
    third = (rest - second.astype(F32)).astype(BF16)
    spread = dot(sel, first) + (dot(sel, second) + dot(sel, third))
    dense[:, :, 0:half] = spread.reshape(zs, 8, half)

    def sum_left(s):
        return pltpu.make_async_remote_copy(
            src_ref=dense.at[n_right - s],
            dst_ref=from_right.at[n_right - 1 - s],
            send_sem=rsend_sem.at[0, s],
            recv_sem=rrecv_sem.at[0, s],
            device_id=z_left,
            device_id_type=MESH,
        )

    def sum_right(s):
        return pltpu.make_async_remote_copy(
            src_ref=dense.at[zs - n_left + s],
            dst_ref=from_left.at[s],
            send_sem=rsend_sem.at[1, s],
            recv_sem=rrecv_sem.at[1, s],
            device_id=z_right,
            device_id_type=MESH,
        )

    tiles = colw // LANES
    per = -(-tiles // max(1, n_right - 1))

    def weight_tile(t):
        side = t // (half // LANES)
        at = pl.multiple_of((t % (half // LANES)) * LANES, LANES)
        down = pl.multiple_of(t * LANES, LANES)
        xs = xd[side, 0, :, :, pl.ds(at, LANES)].reshape(n_slots, LANES)
        ds = xd[side, 1, :, :, pl.ds(at, LANES)].astype(F32)
        scaled = (gate_slot[...] * ds).astype(BF16).reshape(n_slots, LANES)
        both = dot(xs, hid[:, :, 0:256].reshape(n_slots, 256), (0, 0)).astype(BF16)
        gg_buf[pl.ds(down, LANES), :] = both[:, 0:128]
        gu_buf[pl.ds(down, LANES), :] = both[:, 128:256]
        gd_buf[:, pl.ds(down, LANES)] = dot(
            hid[:, :, 256:384].reshape(n_slots, LANES), scaled, (0, 0)
        ).astype(BF16)

    sum_left(0).start()
    if n_left > 0:
        sum_right(0).start()

    def sum_step(s, carry):
        sum_left(s - 1).wait_recv()
        dense[n_right - s] = dense[n_right - s] + from_right[n_right - s]
        sum_left(s).start()

        @pl.when(s < n_left)
        def _():
            sum_right(s - 1).wait_recv()
            dense[zs - n_left + s] = dense[zs - n_left + s] + from_left[s - 1]
            sum_right(s).start()

        for q in range(per):
            t = (s - 1) * per + q

            @pl.when(t < tiles)
            def _():
                weight_tile(t)

        return carry

    if n_right > 1:
        lax.fori_loop(1, n_right, sum_step, 0)
    else:
        lax.fori_loop(0, tiles, lambda t, carry: (weight_tile(t), carry)[1], 0)
    stores = [
        pltpu.make_async_copy(gg_buf, gg_hbm.at[0], local_sem.at[0]),
        pltpu.make_async_copy(gu_buf, gu_hbm.at[0], local_sem.at[1]),
        pltpu.make_async_copy(gd_buf, gd_hbm.at[0], local_sem.at[2]),
    ]
    for store in stores:
        store.start()
    sum_left(n_right - 1).wait_recv()
    final = dense[0] + from_right[0]
    if n_left > 0:
        sum_right(n_left - 1).wait_recv()
        final = final + from_left[n_left - 1]
    gate_grad_ref[...] = final[:, half:]
    last_out[...] = final[:, 0:half]
    end = remote(last_out, last_in, across, keep=False)

    @pl.when(moved)
    def _():
        end.start()
        end.wait_recv()

    @pl.when(jnp.logical_not(moved))
    def _():
        last_in[...] = last_out[...]

    in_grad_ref[...] = last_in[...].astype(BF16)

    @pl.when(moved)
    def _():
        cross.wait_send()
        end.wait_send()

    for copy in sends:
        copy.wait_send()

    def drain_right(s, carry):
        go_right(s).wait_send()
        sum_left(s).wait_send()
        return carry

    def drain_left(s, carry):
        go_left(s).wait_send()
        sum_right(s).wait_send()
        return carry

    lax.fori_loop(0, n_right, drain_right, 0)
    if n_left > 0:
        lax.fori_loop(0, n_left, drain_left, 0)
    for store in stores:
        store.wait()


def body(tokens, out_grad, picks, gates, w_gate, w_up, w_down):
    zs = lax.axis_size("dp")
    width = tokens.shape[1]
    top = picks.shape[1]
    half = width // (2 * RING)
    colw = 2 * half
    toks = 8 * zs
    n_right = zs // 2
    any_spec = pl.BlockSpec(memory_space=pl.ANY)
    vmem_spec = pl.BlockSpec(memory_space=pltpu.VMEM)
    in_grad, gate_grad, gg, gu, gd = pl.pallas_call(
        functools.partial(kernel, (zs, top)),
        out_shape=(
            jax.ShapeDtypeStruct((8, half), BF16),
            jax.ShapeDtypeStruct((8, LANES), F32),
            jax.ShapeDtypeStruct((1, colw, LANES), BF16),
            jax.ShapeDtypeStruct((1, colw, LANES), BF16),
            jax.ShapeDtypeStruct((1, LANES, colw), BF16),
        ),
        in_specs=[vmem_spec] * 4 + [any_spec] * 3,
        out_specs=(vmem_spec, vmem_spec, any_spec, any_spec, any_spec),
        scratch_shapes=[
            pltpu.VMEM((16, half), BF16),
            pltpu.VMEM((16, half), BF16),
            pltpu.VMEM((16, LANES), BF16),
            pltpu.VMEM((RING, 16, LANES), BF16),
            pltpu.VMEM((zs, 16, half + LANES), BF16),
            pltpu.VMEM((toks, LANES), F32),
            pltpu.VMEM((RING, toks, SLOTS), BF16),
            pltpu.VMEM((RING, SLOTS, LANES), F32),
            pltpu.VMEM((2, 2, RING, SLOTS, half), BF16),
            pltpu.VMEM((colw, 2 * LANES), BF16),
            pltpu.VMEM((LANES, colw), BF16),
            pltpu.VMEM((RING, SLOTS, 3 * LANES), F32),
            pltpu.VMEM((3, SLOTS, 3 * LANES), F32),
            pltpu.VMEM((RING, SLOTS, 3 * LANES), BF16),
            pltpu.VMEM((RING * SLOTS, half), BF16),
            pltpu.VMEM((RING * SLOTS, half), BF16),
            pltpu.VMEM((RING, SLOTS, half), F32),
            pltpu.VMEM((RING, SLOTS, half), BF16),
            pltpu.VMEM((3, SLOTS, half), BF16),
            pltpu.VMEM((2 * RING, 8, SLOTS), F32),
            pltpu.VMEM((zs, 8, half + LANES), F32),
            pltpu.VMEM((n_right, 8, half + LANES), F32),
            pltpu.VMEM((n_right, 8, half + LANES), F32),
            pltpu.VMEM((8, half), F32),
            pltpu.VMEM((8, half), F32),
            pltpu.VMEM((colw, LANES), BF16),
            pltpu.VMEM((colw, LANES), BF16),
            pltpu.VMEM((LANES, colw), BF16),
            pltpu.SemaphoreType.DMA((48,)),
            pltpu.SemaphoreType.DMA((48,)),
            pltpu.SemaphoreType.DMA((2, n_right)),
            pltpu.SemaphoreType.DMA((zs,)),
            pltpu.SemaphoreType.DMA((2, n_right)),
            pltpu.SemaphoreType.DMA((2, n_right)),
            pltpu.SemaphoreType.DMA((3,)),
        ],
        compiler_params=pltpu.CompilerParams(
            collective_id=0, has_side_effects=True, vmem_limit_bytes=48 * 1024 * 1024
        ),
    )(tokens, out_grad, picks, gates, w_gate, w_up, w_down)
    return in_grad, gate_grad[:, 0:top], gg, gu, gd


def solution(mesh):
    placed = (
        P(("dp", "local"), None),
        P(("dp", "local"), None),
        P(("dp", "local"), None),
        P(("dp", "local"), None),
        P("dp", None, "node"),
        P("dp", None, "node"),
        P("dp", "node", None),
    )
    return jax.shard_map(
        body,
        mesh=mesh,
        in_specs=placed,
        out_specs=(
            P(("dp", "local"), "node"),
            P(("dp", "local"), None),
            P("dp", "local", "node"),
            P("dp", "local", "node"),
            P("dp", "node", "local"),
        ),
        check_vma=False,
    )
```

```python
import functools

import jax
import jax.numpy as jnp
from jax import lax
from jax.experimental import pallas as pl
from jax.experimental.pallas import tpu as pltpu
from jax.sharding import PartitionSpec as P

F32 = jnp.float32
BF16 = jnp.bfloat16
MESH = pl.DeviceIdType.MESH
SLOTS = 128
RING = 4
LANES = 128


HOP = 5


def plan(zs):
    far, near = zs // 2, -(zs - 1 - zs // 2)
    stops = [0]
    for j in range(1, far // HOP + 1):
        stops += [d for d in (HOP * j, -HOP * j) if near <= d <= far]
    seen = set(stops)
    serves = {}
    for stop in stops:
        serves[stop] = []
        for step in range(1, HOP // 2 + 1):
            for off in (step, -step):
                d = stop + off
                if near <= d <= far and d not in seen:
                    seen.add(d)
                    serves[stop].append(off)
    assert len(seen) == zs
    return stops, serves


def dot(left, right, contract=(1, 0)):
    dims = (((contract[0],), (contract[1],)), ((), ()))
    return lax.dot_general(left, right, dims, preferred_element_type=F32)


def kernel(
    sizes,
    tok_ref,
    dy_ref,
    picks_ref,
    gates_ref,
    wg_hbm,
    wu_hbm,
    wd_hbm,
    in_grad_ref,
    gate_grad_ref,
    gg_ref,
    gu_ref,
    gd_ref,
    own_chunk,
    got_chunk,
    own_meta,
    got_meta,
    ring,
    meta_tok,
    sel_tok,
    gate_slot,
    xd,
    wgu,
    wdn,
    part,
    part_in,
    hid,
    half_out,
    half_in,
    acc,
    acc_out,
    acc_in,
    gate_rows,
    dense,
    dense_out,
    near_in,
    far_in,
    last_out,
    last_in,
    send_sem,
    recv_sem,
    local_sem,
):
    zs, top = sizes
    toks = 8 * zs
    half = own_chunk.shape[1]
    colw = 2 * half
    z = lax.axis_index("dp")
    n = lax.axis_index("node")
    x = lax.axis_index("local")
    y = n // 2
    c = n % 2
    stops, serves = plan(zs)
    offsets = sorted({off for stop in stops for off in serves[stop]} | {HOP, -HOP})
    xr, xl, xo = (x + 1) % RING, (x + 3) % RING, (x + 2) % RING
    yr, yl, yo = (y + 1) % RING, (y + 3) % RING, (y + 2) % RING
    nodes = 2 * RING
    sibling = (z, 2 * y + 1 - c, x)
    y_right, y_left = (z, 2 * yr + c, x), (z, 2 * yl + c, x)
    x_right, x_left = (z, n, xr), (z, n, xl)
    across = (z, 2 * x + c, y)
    moved = x != y

    count = [0]
    sends = []

    def remote(src, dst, device, keep=True):
        i = count[0]
        count[0] += 1
        copy = pltpu.make_async_remote_copy(
            src_ref=src,
            dst_ref=dst,
            send_sem=send_sem.at[i],
            recv_sem=recv_sem.at[i],
            device_id=device,
            device_id_type=MESH,
        )
        if keep:
            sends.append(copy)
        return copy

    row0 = pl.multiple_of(x * colw, LANES)
    loads = [
        pltpu.make_async_copy(
            wg_hbm.at[0, pl.ds(row0, colw), :], wgu.at[:, 0:LANES], local_sem.at[0]
        ),
        pltpu.make_async_copy(
            wu_hbm.at[0, pl.ds(row0, colw), :], wgu.at[:, LANES : 2 * LANES], local_sem.at[1]
        ),
        pltpu.make_async_copy(wd_hbm.at[0, :, pl.ds(row0, colw)], wdn, local_sem.at[2]),
    ]
    for load in loads:
        load.start()

    barrier = pltpu.get_barrier_semaphore()
    peers = [((z + off + zs) % zs, n, x) for off in offsets]
    peers += [(z, n, (x + i) % RING) for i in range(1, RING)]
    peers += [(z, (n + i) % nodes, x) for i in range(1, nodes)]
    for peer in peers:
        pl.semaphore_signal(barrier, inc=1, device_id=peer, device_id_type=MESH)

    @pl.when(moved)
    def _():
        pl.semaphore_signal(barrier, inc=1, device_id=across, device_id_type=MESH)

    col0 = pl.multiple_of(y * colw + c * half, LANES)
    own_chunk[...] = jnp.concatenate(
        [tok_ref[:, pl.ds(col0, half)].astype(F32), dy_ref[:, pl.ds(col0, half)].astype(F32)],
        axis=0,
    ).astype(BF16)
    place = lax.broadcasted_iota(jnp.int32, (top, LANES), 0)
    lane_k = lax.broadcasted_iota(jnp.int32, (top, LANES), 1)
    put_picks = (lane_k == 32 * x + place).astype(F32).astype(BF16)
    put_gates = (lane_k == 32 * x + 8 + place).astype(F32).astype(BF16)
    meta = dot(picks_ref[...].astype(F32).astype(BF16), put_picks) + dot(gates_ref[...], put_gates)
    own_meta[...] = jnp.concatenate([meta, meta], axis=0).astype(BF16)
    got_meta[x] = own_meta[...]

    pl.semaphore_wait(barrier, len(peers) + jnp.where(moved, 1, 0))

    cross = remote(own_chunk, got_chunk, across, keep=False)

    @pl.when(moved)
    def _():
        cross.start()

    @pl.when(jnp.logical_not(moved))
    def _():
        got_chunk[...] = own_chunk[...]

    metas = [
        remote(own_meta, got_meta.at[x], (z, n, (x + i) % RING)) for i in range(1, RING)
    ]
    for copy in metas:
        copy.start()
    for copy in metas:
        copy.wait_recv()
    ring[0, :, half:] = (
        (got_meta[0].astype(F32) + got_meta[1].astype(F32))
        + (got_meta[2].astype(F32) + got_meta[3].astype(F32))
    ).astype(BF16)

    @pl.when(moved)
    def _():
        cross.wait_recv()

    ring[0, :, 0:half] = got_chunk[...]

    coming = {}

    def pass_on(d, off):
        copy = remote(ring.at[d % zs], ring.at[(d + off) % zs], ((z + off + zs) % zs, n, x))
        copy.start()
        coming[d + off] = copy

    for stop in stops:
        if stop != 0:
            coming[stop].wait_recv()
        for step in (HOP, -HOP):
            if stop * step >= 0 and stop + step in stops:
                pass_on(stop, step)
        for off in serves[stop]:
            pass_on(stop, off)
    for d in coming:
        if d not in stops:
            coming[d].wait_recv()

    meta_all = ring[:, :, half:].astype(F32)[:, 0:8, :].reshape(toks, LANES)
    meta_tok[...] = meta_all
    expert = z.astype(F32)
    t_row = lax.broadcasted_iota(jnp.int32, (toks, toks), 0)
    t_col = lax.broadcasted_iota(jnp.int32, (toks, toks), 1)
    before = jnp.logical_and(t_row // 8 == t_col // 8, t_col < t_row).astype(F32).astype(BF16)
    lane = lax.broadcasted_iota(jnp.int32, (toks, LANES), 1)
    t_of = lax.broadcasted_iota(jnp.int32, (toks, LANES), 0)

    def named(group):
        near = jnp.logical_and(lane >= 32 * group, lane < 32 * group + top)
        return jnp.logical_and(meta_all == expert, near)

    def select(group):
        chosen = jnp.sum(named(group).astype(F32), axis=1, keepdims=True)
        chosen = jnp.broadcast_to(chosen, (toks, LANES))
        rank = dot(before, chosen.astype(BF16))
        ok = jnp.logical_and(chosen > 0.5, rank == (lane % 4).astype(F32))
        return jnp.logical_and(ok, t_of // 8 == lane // 4).astype(F32)

    mine = select(y)
    cube = mine.reshape(zs, 8, SLOTS)
    blank = jnp.zeros_like(cube)
    pick_rows = jnp.concatenate(
        [jnp.concatenate([cube, blank], axis=2), jnp.concatenate([blank, cube], axis=2)], axis=1
    ).reshape(16 * zs, 2 * SLOTS)
    rows = ring[:, :, 0:half].reshape(16 * zs, half)
    picked = dot(pick_rows.astype(BF16), rows, (0, 0)).astype(BF16)
    xd[c, 0, y] = picked[0:SLOTS]
    xd[c, 1, y] = picked[SLOTS:]

    to_right = [remote(xd.at[c, p, y], xd.at[c, p, y], y_right) for p in range(2)]
    to_left = [remote(xd.at[c, p, y], xd.at[c, p, y], y_left) for p in range(2)]
    to_core = [remote(xd.at[c, p, y], xd.at[c, p, y], sibling) for p in range(2)]
    on_right = remote(xd.at[c, 0, yl], xd.at[c, 0, yl], y_right)
    on_left = remote(xd.at[c, 1, yr], xd.at[c, 1, yr], y_left)
    core_l = [remote(xd.at[c, p, yl], xd.at[c, p, yl], sibling) for p in range(2)]
    core_r = [remote(xd.at[c, p, yr], xd.at[c, p, yr], sibling) for p in range(2)]
    core_o = [remote(xd.at[c, p, yo], xd.at[c, p, yo], sibling) for p in range(2)]
    to_right[0].start()
    to_left[1].start()
    to_right[1].start()
    to_left[0].start()
    to_core[0].start()
    to_core[1].start()

    rolled = pltpu.roll(meta_all, LANES - 8, 1)
    for group in range(RING):
        chosen = select(group).astype(BF16)
        sel_tok[group] = chosen
        gate_of = jnp.sum(jnp.where(named(group), rolled, 0.0), axis=1, keepdims=True)
        gate_of = jnp.broadcast_to(gate_of, (toks, LANES)).astype(BF16)
        gate_slot[group] = dot(chosen, gate_of, (0, 0))

    to_right[0].wait_recv()
    on_right.start()
    core_l[0].start()
    to_left[1].wait_recv()
    on_left.start()
    core_r[1].start()
    to_right[1].wait_recv()
    core_l[1].start()
    to_left[0].wait_recv()
    core_r[0].start()
    on_right.wait_recv()
    core_o[0].start()
    on_left.wait_recv()
    core_o[1].start()
    for copy in to_core + core_l + core_r + core_o:
        copy.wait_recv()
    for load in loads:
        load.wait()

    n_slots = RING * SLOTS
    gate_up = dot(xd[0, 0].reshape(n_slots, half), wgu[0:half]) + dot(
        xd[1, 0].reshape(n_slots, half), wgu[half:]
    )
    back_part = dot(xd[0, 1].reshape(n_slots, half), wdn[:, 0:half], (1, 1)) + dot(
        xd[1, 1].reshape(n_slots, half), wdn[:, half:], (1, 1)
    )
    part[:, :, 0:256] = gate_up.reshape(RING, SLOTS, 256)
    part[:, :, 256:] = back_part.reshape(RING, SLOTS, LANES)

    lo, hi = slice(0, SLOTS // 2), slice(SLOTS // 2, SLOTS)

    def scatter_copies(src, into, r, l, o, right, left):
        return dict(
            a1=remote(src.at[o, lo], into.at[0, lo], right),
            b1=remote(src.at[o, hi], into.at[0, hi], left),
            a2=remote(src.at[r, hi], into.at[1, hi], right),
            b2=remote(src.at[l, lo], into.at[2, lo], left),
            a3=remote(src.at[r, lo], into.at[1, lo], right),
            b3=remote(src.at[l, hi], into.at[2, hi], left),
        )

    px = scatter_copies(part, part_in, xr, xl, xo, x_right, x_left)
    px["a1"].start()
    px["b1"].start()
    px["a2"].start()
    px["b2"].start()
    px["a1"].wait_recv()
    part[xr, lo] = part[xr, lo] + part_in[0, lo]
    px["a3"].start()
    px["b1"].wait_recv()
    part[xl, hi] = part[xl, hi] + part_in[0, hi]
    px["b3"].start()
    for name in ("a2", "b2", "a3", "b3"):
        px[name].wait_recv()
    summed = part[x] + part_in[1] + part_in[2]

    gate_pre = summed[:, 0:128]
    up_pre = summed[:, 128:256]
    back = summed[:, 256:384]
    gate_col = gate_slot[x]
    sig = jax.nn.sigmoid(gate_pre)
    act = gate_pre * sig * up_pre
    d_act = gate_col * back
    d_up = d_act * gate_pre * sig
    d_pre = d_act * up_pre * sig * (1.0 + gate_pre * (1.0 - sig))
    hid[x, :, 0:128] = d_pre.astype(BF16)
    hid[x, :, 128:256] = d_up.astype(BF16)
    hid[x, :, 256:384] = act.astype(BF16)

    h_right = remote(hid.at[x], hid.at[x], x_right)
    h_left = remote(hid.at[x], hid.at[x], x_left)
    h_on_right = remote(hid.at[xl, lo], hid.at[xl, lo], x_right)
    h_on_left = remote(hid.at[xr, hi], hid.at[xr, hi], x_left)
    h_right.start()
    h_left.start()

    gate_row = jnp.sum(jnp.transpose(back * act), axis=0, keepdims=True)
    gate_rows[n] = jnp.broadcast_to(gate_row, (8, SLOTS))
    rows_out = [
        remote(gate_rows.at[n], gate_rows.at[n], (z, (n + i) % nodes, x)) for i in range(1, nodes)
    ]
    for copy in rows_out:
        copy.start()

    h_right.wait_recv()
    h_on_right.start()
    h_left.wait_recv()
    h_on_left.start()
    h_on_right.wait_recv()
    h_on_left.wait_recv()

    grads = hid[:, :, 0:256].reshape(n_slots, 256)
    other = pl.multiple_of((1 - c) * half, LANES)
    ours = pl.multiple_of(c * half, LANES)
    half_out[...] = dot(grads, wgu[pl.ds(other, half), :], (1, 1)).astype(BF16)
    core_half = remote(half_out, half_in, sibling)
    core_half.start()
    acc[...] = dot(grads, wgu[pl.ds(ours, half), :], (1, 1)).reshape(RING, SLOTS, half)
    core_half.wait_recv()
    arrived = half_in[...].astype(F32).reshape(RING, SLOTS, half)
    acc[...] = acc[...] + arrived

    py = scatter_copies(acc_out, acc_in, yr, yl, yo, y_right, y_left)
    acc_out[yo] = acc[yo].astype(BF16)
    py["a1"].start()
    py["b1"].start()
    acc_out[yr, hi] = acc[yr, hi].astype(BF16)
    py["a2"].start()
    acc_out[yl, lo] = acc[yl, lo].astype(BF16)
    py["b2"].start()

    for copy in rows_out:
        copy.wait_recv()
    gate_sum = gate_rows[0]
    for i in range(1, nodes):
        gate_sum = gate_sum + gate_rows[i]
    gate_tok = jnp.sum(sel_tok[x].astype(F32) * gate_sum[0:1], axis=1, keepdims=True)
    meta_x = jnp.zeros((toks, LANES), F32)
    for i in range(RING):
        turned = meta_tok[...] if i == 0 else pltpu.roll(meta_tok[...], LANES - 32 * i, 1)
        meta_x = jnp.where(x == i, turned, meta_x)
    hit = jnp.logical_and(meta_x == expert, lane < top)
    gate_hi = gate_tok.astype(BF16).astype(F32)
    gate_tile = jnp.where(hit, gate_hi, 0.0) + pltpu.roll(
        jnp.where(hit, gate_tok - gate_hi, 0.0), LANES // 2, 1
    )

    py["a1"].wait_recv()
    acc_out[yr, lo] = (acc[yr, lo] + acc_in[0, lo].astype(F32)).astype(BF16)
    py["a3"].start()
    py["b1"].wait_recv()
    acc_out[yl, hi] = (acc[yl, hi] + acc_in[0, hi].astype(F32)).astype(BF16)
    py["b3"].start()
    for name in ("a2", "b2", "a3", "b3"):
        py[name].wait_recv()
    total = acc[y] + acc_in[1].astype(F32) + acc_in[2].astype(F32)

    sel = sel_tok[y]
    first = total.astype(BF16)
    rest = total - first.astype(F32)
    second = rest.astype(BF16)
    third = (rest - second.astype(F32)).astype(BF16)
    spread = dot(sel, first) + (dot(sel, second) + dot(sel, third))
    full = jnp.concatenate([spread, gate_tile], axis=1)
    wide = (half + LANES) // 2
    dense[:, 0:8, :] = full[:, 0:wide].reshape(zs, 8, wide)
    dense[:, 8:16, :] = full[:, wide:].reshape(zs, 8, wide)
    dense_out[...] = dense[...].astype(BF16)

    near = {}
    for stop in reversed(stops):
        for off in serves[stop]:
            near[stop, off] = remote(
                dense_out.at[(stop + off) % zs],
                near_in.at[len(near)],
                ((z - off + zs) % zs, n, x),
            )
            near[stop, off].start()
    slot_of = {key: i for i, key in enumerate(near)}

    tiles = colw // LANES
    def weight_tile(t):
        side = t // (half // LANES)
        at = pl.multiple_of((t % (half // LANES)) * LANES, LANES)
        down = pl.multiple_of(t * LANES, LANES)
        xs = xd[side, 0, :, :, pl.ds(at, LANES)].reshape(n_slots, LANES)
        ds = xd[side, 1, :, :, pl.ds(at, LANES)].astype(F32)
        scaled = (gate_slot[...] * ds).astype(BF16).reshape(n_slots, LANES)
        both = dot(xs, hid[:, :, 0:256].reshape(n_slots, 256), (0, 0)).astype(BF16)
        gg_ref[0, pl.ds(down, LANES), :] = both[:, 0:128]
        gu_ref[0, pl.ds(down, LANES), :] = both[:, 128:256]
        gd_ref[0, :, pl.ds(down, LANES)] = dot(
            hid[:, :, 256:384].reshape(n_slots, LANES), scaled, (0, 0)
        ).astype(BF16)

    def weight_tiles(first, last):
        def one(t, carry):
            weight_tile(t)
            return carry

        lax.fori_loop(first, last, one, 0)

    levels = len(stops) // 2
    share = -(-tiles // (levels + 1))
    weight_tiles(0, min(share, tiles))
    far = {}
    for i, stop in enumerate(reversed(stops)):
        value = dense[stop % zs]
        for off in serves[stop]:
            near[stop, off].wait_recv()
            value = value + near_in[slot_of[stop, off]].astype(F32)
        for step in (HOP, -HOP):
            if stop * step >= 0 and stop + step in stops:
                far[stop + step].wait_recv()
                value = value + far_in[stops.index(stop + step) - 1].astype(F32)
        if stop == 0:
            final = value
        else:
            dense_out[stop % zs] = value.astype(BF16)
            back_by = HOP if stop > 0 else -HOP
            far[stop] = remote(
                dense_out.at[stop % zs],
                far_in.at[stops.index(stop) - 1],
                ((z - back_by + zs) % zs, n, x),
            )
            far[stop].start()
            if i % 2 == 1:
                done = share * ((i + 1) // 2)
                weight_tiles(min(done, tiles), min(done + share, tiles))
    final = jnp.concatenate([final[0:8], final[8:16]], axis=1)
    gate_both = final[:, half:]
    gate_grad_ref[...] = gate_both + pltpu.roll(gate_both, LANES // 2, 1)
    last_out[...] = final[:, 0:half]
    end = remote(last_out, last_in, across, keep=False)

    @pl.when(moved)
    def _():
        end.start()
        end.wait_recv()

    @pl.when(jnp.logical_not(moved))
    def _():
        last_in[...] = last_out[...]

    in_grad_ref[...] = last_in[...].astype(BF16)

    @pl.when(moved)
    def _():
        cross.wait_send()
        end.wait_send()

    for copy in sends:
        copy.wait_send()


def body(tokens, out_grad, picks, gates, w_gate, w_up, w_down):
    zs = lax.axis_size("dp")
    width = tokens.shape[1]
    top = picks.shape[1]
    half = width // (2 * RING)
    colw = 2 * half
    toks = 8 * zs
    wide = (half + LANES) // 2
    stops, _ = plan(zs)
    hbm_spec = pl.BlockSpec(memory_space=pltpu.HBM)
    vmem_spec = pl.BlockSpec(memory_space=pltpu.VMEM)
    in_grad, gate_grad, gg, gu, gd = pl.pallas_call(
        functools.partial(kernel, (zs, top)),
        out_shape=(
            jax.ShapeDtypeStruct((8, half), BF16),
            jax.ShapeDtypeStruct((8, LANES), F32),
            jax.ShapeDtypeStruct((1, colw, LANES), BF16),
            jax.ShapeDtypeStruct((1, colw, LANES), BF16),
            jax.ShapeDtypeStruct((1, LANES, colw), BF16),
        ),
        in_specs=[vmem_spec] * 4 + [hbm_spec] * 3,
        out_specs=(vmem_spec,) * 5,
        scratch_shapes=[
            pltpu.VMEM((16, half), BF16),
            pltpu.VMEM((16, half), BF16),
            pltpu.VMEM((16, LANES), BF16),
            pltpu.VMEM((RING, 16, LANES), BF16),
            pltpu.VMEM((zs, 16, half + LANES), BF16),
            pltpu.VMEM((toks, LANES), F32),
            pltpu.VMEM((RING, toks, SLOTS), BF16),
            pltpu.VMEM((RING, SLOTS, LANES), F32),
            pltpu.VMEM((2, 2, RING, SLOTS, half), BF16),
            pltpu.VMEM((colw, 2 * LANES), BF16),
            pltpu.VMEM((LANES, colw), BF16),
            pltpu.VMEM((RING, SLOTS, 3 * LANES), F32),
            pltpu.VMEM((3, SLOTS, 3 * LANES), F32),
            pltpu.VMEM((RING, SLOTS, 3 * LANES), BF16),
            pltpu.VMEM((RING * SLOTS, half), BF16),
            pltpu.VMEM((RING * SLOTS, half), BF16),
            pltpu.VMEM((RING, SLOTS, half), F32),
            pltpu.VMEM((RING, SLOTS, half), BF16),
            pltpu.VMEM((3, SLOTS, half), BF16),
            pltpu.VMEM((2 * RING, 8, SLOTS), F32),
            pltpu.VMEM((zs, 16, wide), F32),
            pltpu.VMEM((zs, 16, wide), BF16),
            pltpu.VMEM((zs - len(stops), 16, wide), BF16),
            pltpu.VMEM((len(stops) - 1, 16, wide), BF16),
            pltpu.VMEM((8, half), F32),
            pltpu.VMEM((8, half), F32),
            pltpu.SemaphoreType.DMA((48 + 2 * zs,)),
            pltpu.SemaphoreType.DMA((48 + 2 * zs,)),
            pltpu.SemaphoreType.DMA((3,)),
        ],
        compiler_params=pltpu.CompilerParams(
            collective_id=0, has_side_effects=True, vmem_limit_bytes=60 * 1024 * 1024
        ),
    )(tokens, out_grad, picks, gates, w_gate, w_up, w_down)
    return in_grad, gate_grad[:, 0:top], gg, gu, gd


def solution(mesh):
    placed = (
        P(("dp", "local"), None),
        P(("dp", "local"), None),
        P(("dp", "local"), None),
        P(("dp", "local"), None),
        P("dp", None, "node"),
        P("dp", None, "node"),
        P("dp", "node", None),
    )
    return jax.shard_map(
        body,
        mesh=mesh,
        in_specs=placed,
        out_specs=(
            P(("dp", "local"), "node"),
            P(("dp", "local"), None),
            P("dp", "local", "node"),
            P("dp", "local", "node"),
            P("dp", "node", "local"),
        ),
        check_vma=False,
    )
```

```python
import functools

import jax
import jax.numpy as jnp
from jax import lax
from jax.experimental import pallas as pl
from jax.experimental.pallas import tpu as pltpu
from jax.sharding import PartitionSpec as P

F32 = jnp.float32
BF16 = jnp.bfloat16
MESH = pl.DeviceIdType.MESH
SLOTS = 128
RING = 4
LANES = 128
FIRST, MIDDLE, LATE = (0, 64), (64, 96), (96, 128)
EARLY = (0, 96)


HOP = 5


def plan(zs):
    far, near = zs // 2, -(zs - 1 - zs // 2)
    stops = [0]
    for j in range(1, far // HOP + 1):
        stops += [d for d in (HOP * j, -HOP * j) if near <= d <= far]
    seen = set(stops)
    serves = {}
    for stop in stops:
        serves[stop] = []
        for step in range(1, HOP // 2 + 1):
            for off in (step, -step):
                d = stop + off
                if near <= d <= far and d not in seen:
                    seen.add(d)
                    serves[stop].append(off)
    assert len(seen) == zs
    return stops, serves


def dot(left, right, contract=(1, 0)):
    dims = (((contract[0],), (contract[1],)), ((), ()))
    return lax.dot_general(left, right, dims, preferred_element_type=F32)


def kernel(
    sizes,
    tok_ref,
    dy_ref,
    picks_ref,
    gates_ref,
    wg_hbm,
    wu_hbm,
    wd_hbm,
    in_grad_ref,
    gate_grad_ref,
    gg_ref,
    gu_ref,
    gd_ref,
    own_chunk,
    packs,
    ring,
    meta_tok,
    sel_tok,
    gate_slot,
    xd,
    wgu,
    wdn,
    part,
    part_in,
    hid,
    half_out,
    half_in,
    acc,
    acc_out,
    acc_in,
    own_gate,
    gate_rows,
    dense,
    dense_out,
    near_in,
    far_in,
    last_in,
    send_sem,
    recv_sem,
    local_sem,
):
    zs, top = sizes
    toks = 8 * zs
    half = own_chunk.shape[1] - LANES
    colw = 2 * half
    z = lax.axis_index("dp")
    n = lax.axis_index("node")
    x = lax.axis_index("local")
    y = n // 2
    c = n % 2
    stops, serves = plan(zs)
    n_first, n_early = zs // 2, 3 * zs // 4
    order = sorted(range(zs // 2 + 1 - zs, zs // 2 + 1), key=lambda d: (abs(d), -d))
    at = order.index

    offsets = sorted({off for stop in stops for off in serves[stop]} | {HOP, -HOP})
    xr, xl, xo = (x + 1) % RING, (x + 3) % RING, (x + 2) % RING
    yr, yl, yo = (y + 1) % RING, (y + 3) % RING, (y + 2) % RING
    nodes = 2 * RING
    sibling = (z, 2 * y + 1 - c, x)
    y_right, y_left = (z, 2 * yr + c, x), (z, 2 * yl + c, x)
    x_right, x_left, x_over = (z, n, xr), (z, n, xl), (z, n, xo)
    y_over = (z, 2 * yo + c, x)
    moved = x != y

    def across(off):
        return ((z + off + zs) % zs, 2 * x + c, y)

    gate_to = [(z, 2 * x + (c + i % 2) % 2, (x + i // 2) % RING) for i in range(nodes)]
    gate_from = [(z, (n + i) % nodes, y) for i in range(nodes)]

    count = [0]
    sends = []

    def remote(src, dst, device, keep=True):
        i = count[0]
        count[0] += 1
        copy = pltpu.make_async_remote_copy(
            src_ref=src,
            dst_ref=dst,
            send_sem=send_sem.at[i],
            recv_sem=recv_sem.at[i],
            device_id=device,
            device_id_type=MESH,
        )
        if keep:
            sends.append(copy)
        return copy

    row0 = pl.multiple_of(x * colw, LANES)
    loads = [
        pltpu.make_async_copy(
            wg_hbm.at[0, pl.ds(row0, colw), :], wgu.at[:, 0:LANES], local_sem.at[0]
        ),
        pltpu.make_async_copy(
            wu_hbm.at[0, pl.ds(row0, colw), :], wgu.at[:, LANES : 2 * LANES], local_sem.at[1]
        ),
        pltpu.make_async_copy(wd_hbm.at[0, :, pl.ds(row0, colw)], wdn, local_sem.at[2]),
    ]
    for load in loads:
        load.start()

    barrier = pltpu.get_barrier_semaphore()
    peers = [((z + off + zs) % zs, n, x) for off in offsets]
    peers += [(z, n, (x + i) % RING) for i in range(1, RING)]
    peers += [y_right, y_left, y_over, sibling] + gate_from[1:]
    peers += [across(off) for off in offsets]
    for peer in peers:
        pl.semaphore_signal(barrier, inc=1, device_id=peer, device_id_type=MESH)

    @pl.when(moved)
    def _():
        for peer in (across(0), gate_from[0]):
            pl.semaphore_signal(barrier, inc=1, device_id=peer, device_id_type=MESH)

    col0 = pl.multiple_of(y * colw + c * half, LANES)
    own_chunk[:, 0:half] = jnp.concatenate(
        [tok_ref[:, pl.ds(col0, half)].astype(F32), dy_ref[:, pl.ds(col0, half)].astype(F32)],
        axis=0,
    ).astype(BF16)
    place = lax.broadcasted_iota(jnp.int32, (top, LANES), 0)
    lane_k = lax.broadcasted_iota(jnp.int32, (top, LANES), 1)
    put_picks = (lane_k == place).astype(F32).astype(BF16)
    put_gates = (lane_k == 8 + place).astype(F32).astype(BF16)
    meta = dot(picks_ref[...].astype(F32).astype(BF16), put_picks) + dot(gates_ref[...], put_gates)
    own_chunk[:, half:] = jnp.concatenate([meta, meta], axis=0).astype(BF16)

    pl.semaphore_wait(barrier, len(peers) + jnp.where(moved, 2, 0))

    coming = {}
    cross = remote(own_chunk, ring.at[at(0)], across(0), keep=False)

    def pass_on(d, off):
        if d == 0:
            copy = remote(own_chunk, ring.at[at(off)], across(off))
        else:
            copy = remote(ring.at[at(d)], ring.at[at(d + off)], ((z + off + zs) % zs, n, x))
        copy.start()
        coming[d + off] = copy

    def start_cross():
        @pl.when(moved)
        def _():
            cross.start()

        @pl.when(jnp.logical_not(moved))
        def _():
            ring[at(0)] = own_chunk[...]

    for stop in stops:
        if stop != 0:
            coming[stop].wait_recv()
        for step in (HOP, -HOP):
            if stop * step >= 0 and stop + step in stops:
                pass_on(stop, step)
        for off in serves[stop]:
            pass_on(stop, off)
        if stop == 0:
            start_cross()

    @pl.when(moved)
    def _():
        cross.wait_recv()

    expert = z.astype(F32)

    def counts(shape, axis):
        return lax.broadcasted_iota(jnp.int32, shape, axis)

    def named(metas):
        return jnp.logical_and(metas == expert, counts(metas.shape, 1) < top)

    def select(metas, first):
        tall = metas.shape[0]
        t_row, t_col = counts((tall, tall), 0), counts((tall, tall), 1)
        before = jnp.logical_and(t_row // 8 == t_col // 8, t_col < t_row).astype(F32).astype(BF16)
        lane = counts(metas.shape, 1)
        chunk = first + counts(metas.shape, 0) // 8
        home = jnp.where(chunk < n_first, chunk, chunk - n_first + MIDDLE[0] // 4)
        home = jnp.where(chunk < n_early, home, chunk - n_early + LATE[0] // 4)
        chosen = jnp.sum(named(metas).astype(F32), axis=1, keepdims=True)
        chosen = jnp.broadcast_to(chosen, metas.shape)
        rank = dot(before, chosen.astype(BF16))
        ok = jnp.logical_and(chosen > 0.5, rank == (lane % 4).astype(F32))
        return jnp.logical_and(ok, home == lane // 4).astype(F32)

    def pieces(batch):
        rows = slice(*batch)

        def move(p, group, device):
            ref = xd.at[c, p, group, rows]
            return remote(ref, ref, device)

        copies = dict(
            right=[move(p, y, y_right) for p in range(2)],
            left=[move(p, y, y_left) for p in range(2)],
            core=[move(p, y, sibling) for p in range(2)],
            core_l=[move(p, yl, sibling) for p in range(2)],
            core_r=[move(p, yr, sibling) for p in range(2)],
            core_o=[move(p, yo, sibling) for p in range(2)],
        )
        if batch == LATE:
            copies["over"] = [move(p, y, y_over) for p in range(2)]
        else:
            copies["on_right"] = move(0, yl, y_right)
            copies["on_left"] = move(1, yr, y_left)
        return copies

    def send_picked(batch, first, last):
        number = last - first
        for d in coming:
            if d not in stops and first <= at(d) < last:
                coming[d].wait_recv()
        metas = ring[first:last, :, half:].astype(F32)[:, 0:8, :].reshape(8 * number, LANES)
        meta_tok[y, 8 * first : 8 * last] = metas
        cube = select(metas, first).reshape(number, 8, SLOTS)
        blank = jnp.zeros_like(cube)
        pick_rows = jnp.concatenate(
            [jnp.concatenate([cube, blank], axis=2), jnp.concatenate([blank, cube], axis=2)],
            axis=1,
        ).reshape(16 * number, 2 * SLOTS)
        chunks = ring[first:last, :, 0:half].reshape(16 * number, half)
        picked = dot(pick_rows.astype(BF16), chunks, (0, 0)).astype(BF16)
        lo, hi = batch
        xd[c, 0, y, lo:hi] = picked[lo:hi]
        xd[c, 1, y, lo:hi] = picked[SLOTS + lo : SLOTS + hi]
        copies = pieces(batch)
        for copy in copies.get("over", []):
            copy.start()
        copies["right"][0].start()
        copies["left"][1].start()
        copies["right"][1].start()
        copies["left"][0].start()
        copies["core"][0].start()
        copies["core"][1].start()
        return copies

    def relay_picked(copies):
        for p in range(2):
            copies["right"][p].wait_recv()
            if p == 0 and "on_right" in copies:
                copies["on_right"].start()
            copies["core_l"][p].start()
            copies["left"][1 - p].wait_recv()
            if p == 0 and "on_left" in copies:
                copies["on_left"].start()
            copies["core_r"][1 - p].start()

    def finish_picked(copies):
        far = copies["over"] if "over" in copies else [copies["on_right"], copies["on_left"]]
        for p in range(2):
            far[p].wait_recv()
            copies["core_o"][p].start()

    def end_picked(copies):
        for name in ("core", "core_l", "core_r", "core_o"):
            for copy in copies[name]:
                copy.wait_recv()

    early = send_picked(FIRST, 0, n_first)
    middle = send_picked(MIDDLE, n_first, n_early)
    relay_picked(early)
    late = send_picked(LATE, n_early, zs)

    tall = packs.shape[1]
    mine = meta_tok[y]
    if 8 * tall > toks:
        mine = jnp.concatenate([mine, jnp.zeros((8 * tall - toks, LANES), F32)], axis=0)
    packed = mine[0:tall]
    for i in range(1, 8):
        packed = packed + pltpu.roll(mine[i * tall : (i + 1) * tall], 16 * i, 1)
    packs[y] = packed.astype(BF16)
    packs_out = [remote(packs.at[y], packs.at[y], peer) for peer in (y_over, y_right, y_left)]
    for copy in packs_out:
        copy.start()
    relay_picked(middle)
    finish_picked(early)
    relay_picked(late)

    sel_tok[...] = select(meta_tok[y], 0).astype(BF16)
    for copy in packs_out:
        copy.wait_recv()
    for group in range(RING):
        pack = packs[group].astype(F32)
        metas = jnp.concatenate(
            [pack] + [pltpu.roll(pack, LANES - 16 * i, 1) for i in range(1, 8)], axis=0
        )[0:toks]
        chosen = select(metas, 0).astype(BF16)
        gate_of = jnp.where(named(metas), pltpu.roll(metas, LANES - 8, 1), 0.0)
        gate_of = jnp.sum(gate_of, axis=1, keepdims=True)
        gate_of = jnp.broadcast_to(gate_of, (toks, LANES)).astype(BF16)
        gate_slot[group] = dot(chosen, gate_of, (0, 0))

    for load in loads:
        load.wait()
    finish_picked(middle)
    end_picked(early)
    end_picked(middle)

    n_slots = RING * SLOTS

    def halves(batch):
        first, last = batch
        middle = (first + last) // 2
        return slice(first, middle), slice(middle, last)

    def scatter_copies(batch, src, into, r, l, o, right, left, over):
        if batch == LATE:
            rows = slice(*batch)
            return dict(
                far=remote(src.at[o, rows], into.at[0, rows], over),
                right=remote(src.at[r, rows], into.at[1, rows], right),
                left=remote(src.at[l, rows], into.at[2, rows], left),
            )
        lo, hi = halves(batch)
        return dict(
            a1=remote(src.at[o, lo], into.at[0, lo], right),
            b1=remote(src.at[o, hi], into.at[0, hi], left),
            a2=remote(src.at[r, hi], into.at[1, hi], right),
            b2=remote(src.at[l, lo], into.at[2, lo], left),
            a3=remote(src.at[r, lo], into.at[1, lo], right),
            b3=remote(src.at[l, hi], into.at[2, hi], left),
        )

    def send_partial(batch):
        first, last = batch
        tall = RING * (last - first)

        def take(side, p):
            return xd[side, p, :, first:last, :].reshape(tall, half)

        gate_up = dot(take(0, 0), wgu[0:half]) + dot(take(1, 0), wgu[half:])
        back_part = dot(take(0, 1), wdn[:, 0:half], (1, 1)) + dot(
            take(1, 1), wdn[:, half:], (1, 1)
        )
        part[:, first:last, 0:256] = gate_up.reshape(RING, last - first, 256)
        part[:, first:last, 256:] = back_part.reshape(RING, last - first, LANES)
        copies = scatter_copies(batch, part, part_in, xr, xl, xo, x_right, x_left, x_over)
        for name in ("far", "right", "left") if batch == LATE else ("a1", "b1", "a2", "b2"):
            copies[name].start()
        return copies

    def relay_partial(copies, batch):
        lo, hi = halves(batch)
        copies["a1"].wait_recv()
        part[xr, lo] = part[xr, lo] + part_in[0, lo]
        copies["a3"].start()
        copies["b1"].wait_recv()
        part[xl, hi] = part[xl, hi] + part_in[0, hi]
        copies["b3"].start()

    def send_hidden(copies, batch):
        rows = slice(*batch)
        for name in ("far", "right", "left") if batch == LATE else ("a2", "b2", "a3", "b3"):
            copies[name].wait_recv()
        summed = part[x, rows] + part_in[1, rows] + part_in[2, rows]
        if batch == LATE:
            summed = summed + part_in[0, rows]
        gate_pre = summed[:, 0:128]
        up_pre = summed[:, 128:256]
        back = summed[:, 256:384]
        gate_col = gate_slot[x, rows]
        sig = jax.nn.sigmoid(gate_pre)
        act = gate_pre * sig * up_pre
        d_act = gate_col * back
        d_up = d_act * gate_pre * sig
        d_pre = d_act * up_pre * sig * (1.0 + gate_pre * (1.0 - sig))
        hid[x, rows, 0:128] = d_pre.astype(BF16)
        hid[x, rows, 128:256] = d_up.astype(BF16)
        hid[x, rows, 256:384] = act.astype(BF16)
        mine = hid.at[x, rows]
        moves = [remote(mine, mine, x_right), remote(mine, mine, x_left)]
        if batch == LATE:
            moves.append(remote(mine, mine, x_over))
        for move in moves:
            move.start()
        if batch != LATE:
            lo, hi = halves(batch)
            moves.append(remote(hid.at[xl, lo], hid.at[xl, lo], x_right))
            moves.append(remote(hid.at[xr, hi], hid.at[xr, hi], x_left))
        return moves, back * act

    def relay_hidden(moves):
        moves[0].wait_recv()
        moves[2].start()
        moves[1].wait_recv()
        moves[3].start()

    px_early = send_partial(EARLY)
    finish_picked(late)
    relay_partial(px_early, EARLY)
    end_picked(late)
    px_late = send_partial(LATE)
    h_early, gates_early = send_hidden(px_early, EARLY)
    relay_hidden(h_early)
    h_late, gates_late = send_hidden(px_late, LATE)

    gate_parts = jnp.concatenate([gates_early, gates_late], axis=0)
    gate_row = jnp.sum(jnp.transpose(gate_parts), axis=0, keepdims=True)
    own_gate[...] = jnp.broadcast_to(gate_row, (8, SLOTS))
    first_gate = count[0]
    count[0] += nodes

    def gate_copy(i, sender):
        return pltpu.make_async_remote_copy(
            src_ref=own_gate,
            dst_ref=gate_rows.at[sender],
            send_sem=send_sem.at[first_gate + i],
            recv_sem=recv_sem.at[first_gate + sender],
            device_id=gate_to[i],
            device_id_type=MESH,
        )

    gate_out = [gate_copy(i, n) for i in range(nodes)]

    @pl.when(moved)
    def _():
        gate_out[0].start()

    @pl.when(jnp.logical_not(moved))
    def _():
        gate_rows[n] = own_gate[...]

    for copy in gate_out[1:]:
        copy.start()

    for copy in h_early[2:] + h_late:
        copy.wait_recv()

    grads = hid[:, :, 0:256].reshape(n_slots, 256)
    other = pl.multiple_of((1 - c) * half, LANES)
    ours = pl.multiple_of(c * half, LANES)
    half_out[...] = (
        dot(grads, wgu[pl.ds(other, half), :], (1, 1)).astype(BF16).reshape(RING, SLOTS, half)
    )
    core_half = {}
    for batch in (LATE, EARLY):
        rows = slice(*batch)
        core_half[batch] = remote(half_out.at[:, rows], half_in.at[:, rows], sibling)
        core_half[batch].start()
    acc[...] = dot(grads, wgu[pl.ds(ours, half), :], (1, 1)).reshape(RING, SLOTS, half)

    py = {}
    for batch in (LATE, EARLY):
        rows = slice(*batch)
        lo, hi = halves(batch)
        core_half[batch].wait_recv()
        acc[:, rows] = acc[:, rows] + half_in[:, rows].astype(F32)
        py[batch] = scatter_copies(batch, acc_out, acc_in, yr, yl, yo, y_right, y_left, y_over)
        acc_out[yo, rows] = acc[yo, rows].astype(BF16)
        if batch == LATE:
            py[batch]["far"].start()
            acc_out[yr, rows] = acc[yr, rows].astype(BF16)
            py[batch]["right"].start()
            acc_out[yl, rows] = acc[yl, rows].astype(BF16)
            py[batch]["left"].start()
        else:
            py[batch]["a1"].start()
            py[batch]["b1"].start()
            acc_out[yr, hi] = acc[yr, hi].astype(BF16)
            py[batch]["a2"].start()
            acc_out[yl, lo] = acc[yl, lo].astype(BF16)
            py[batch]["b2"].start()

    for sender in range(nodes):

        @pl.when(jnp.logical_or(moved, n != sender))
        def _():
            gate_copy(0, sender).wait_recv()

    gate_sum = gate_rows[0]
    for i in range(1, nodes):
        gate_sum = gate_sum + gate_rows[i]
    gate_tok = jnp.sum(sel_tok[...].astype(F32) * gate_sum[0:1], axis=1, keepdims=True)
    hit = named(meta_tok[y])
    gate_hi = gate_tok.astype(BF16).astype(F32)
    gate_tile = jnp.where(hit, gate_hi, 0.0) + pltpu.roll(
        jnp.where(hit, gate_tok - gate_hi, 0.0), LANES // 2, 1
    )

    def relay_sums(batch):
        lo, hi = halves(batch)
        py[batch]["a1"].wait_recv()
        acc_out[yr, lo] = (acc[yr, lo] + acc_in[0, lo].astype(F32)).astype(BF16)
        py[batch]["a3"].start()
        py[batch]["b1"].wait_recv()
        acc_out[yl, hi] = (acc[yl, hi] + acc_in[0, hi].astype(F32)).astype(BF16)
        py[batch]["b3"].start()

    wide = (half + LANES) // 2

    def spread_sums(batch, first, last):
        rows = slice(*batch)
        for name in ("far", "right", "left") if batch == LATE else ("a2", "b2", "a3", "b3"):
            py[batch][name].wait_recv()
        total = acc[y, rows] + acc_in[1, rows].astype(F32) + acc_in[2, rows].astype(F32)
        if batch == LATE:
            total = total + acc_in[0, rows].astype(F32)
        blank = jnp.zeros((SLOTS - (batch[1] - batch[0]), half), F32)
        total = jnp.concatenate([total, blank] if batch == EARLY else [blank, total], axis=0)
        sel = sel_tok[8 * first : 8 * last]
        one = total.astype(BF16)
        rest = total - one.astype(F32)
        two = rest.astype(BF16)
        three = (rest - two.astype(F32)).astype(BF16)
        spread = dot(sel, one) + (dot(sel, two) + dot(sel, three))
        full = jnp.concatenate([spread, gate_tile[8 * first : 8 * last]], axis=1)
        dense[first:last, 0:8, :] = full[:, 0:wide].reshape(last - first, 8, wide)
        dense[first:last, 8:16, :] = full[:, wide:].reshape(last - first, 8, wide)
        dense_out[first:last] = dense[first:last].astype(BF16)

    near = {}

    def send_near(first, last):
        for stop in reversed(stops):
            for off in serves[stop]:
                if first <= at(stop + off) < last:
                    near[stop, off] = remote(
                        dense_out.at[at(stop + off)],
                        near_in.at[len(near)],
                        across(-off) if stop == 0 else ((z - off + zs) % zs, n, x),
                    )
                    near[stop, off].start()

    spread_sums(LATE, n_early, zs)
    send_near(n_early, zs)
    relay_sums(EARLY)
    spread_sums(EARLY, 0, n_early)
    send_near(0, n_early)
    end = remote(dense_out.at[at(0)], last_in, across(0), keep=False)

    @pl.when(moved)
    def _():
        end.start()

    @pl.when(jnp.logical_not(moved))
    def _():
        last_in[...] = dense_out[at(0)]

    slot_of = {key: i for i, key in enumerate(near)}

    tiles = colw // LANES
    def weight_tile(t):
        side = t // (half // LANES)
        left = pl.multiple_of((t % (half // LANES)) * LANES, LANES)
        down = pl.multiple_of(t * LANES, LANES)
        xs = xd[side, 0, :, :, pl.ds(left, LANES)].reshape(n_slots, LANES)
        ds = xd[side, 1, :, :, pl.ds(left, LANES)].astype(F32)
        scaled = (gate_slot[...] * ds).astype(BF16).reshape(n_slots, LANES)
        both = dot(xs, hid[:, :, 0:256].reshape(n_slots, 256), (0, 0)).astype(BF16)
        gg_ref[0, pl.ds(down, LANES), :] = both[:, 0:128]
        gu_ref[0, pl.ds(down, LANES), :] = both[:, 128:256]
        gd_ref[0, :, pl.ds(down, LANES)] = dot(
            hid[:, :, 256:384].reshape(n_slots, LANES), scaled, (0, 0)
        ).astype(BF16)

    def weight_tiles(first, last):
        def one(t, carry):
            weight_tile(t)
            return carry

        lax.fori_loop(first, last, one, 0)

    levels = len(stops) // 2
    share = -(-tiles // (levels + 1))
    weight_tiles(0, min(share, tiles))
    far = {}
    for i, stop in enumerate(reversed(stops)):
        if stop == 0:

            @pl.when(moved)
            def _():
                end.wait_recv()

        value = last_in[...].astype(F32) if stop == 0 else dense[at(stop)]
        for off in serves[stop]:
            near[stop, off].wait_recv()
            value = value + near_in[slot_of[stop, off]].astype(F32)
        for step in (HOP, -HOP):
            if stop * step >= 0 and stop + step in stops:
                far[stop + step].wait_recv()
                value = value + far_in[stops.index(stop + step) - 1].astype(F32)
        if stop == 0:
            final = value
        else:
            dense_out[at(stop)] = value.astype(BF16)
            back_by = HOP if stop > 0 else -HOP
            far[stop] = remote(
                dense_out.at[at(stop)],
                far_in.at[stops.index(stop) - 1],
                across(-back_by) if stop == back_by else ((z - back_by + zs) % zs, n, x),
            )
            far[stop].start()
            if i % 2 == 1:
                done = share * ((i + 1) // 2)
                weight_tiles(min(done, tiles), min(done + share, tiles))
    final = jnp.concatenate([final[0:8], final[8:16]], axis=1)
    gate_both = final[:, half:]
    gate_grad_ref[...] = gate_both + pltpu.roll(gate_both, LANES // 2, 1)
    in_grad_ref[...] = final[:, 0:half].astype(BF16)

    @pl.when(moved)
    def _():
        cross.wait_send()
        end.wait_send()
        gate_out[0].wait_send()

    for copy in gate_out[1:]:
        copy.wait_send()

    for copy in sends:
        copy.wait_send()


def body(tokens, out_grad, picks, gates, w_gate, w_up, w_down):
    zs = lax.axis_size("dp")
    width = tokens.shape[1]
    top = picks.shape[1]
    half = width // (2 * RING)
    colw = 2 * half
    toks = 8 * zs
    wide = (half + LANES) // 2
    stops, _ = plan(zs)
    hbm_spec = pl.BlockSpec(memory_space=pltpu.HBM)
    vmem_spec = pl.BlockSpec(memory_space=pltpu.VMEM)
    in_grad, gate_grad, gg, gu, gd = pl.pallas_call(
        functools.partial(kernel, (zs, top)),
        out_shape=(
            jax.ShapeDtypeStruct((8, half), BF16),
            jax.ShapeDtypeStruct((8, LANES), F32),
            jax.ShapeDtypeStruct((1, colw, LANES), BF16),
            jax.ShapeDtypeStruct((1, colw, LANES), BF16),
            jax.ShapeDtypeStruct((1, LANES, colw), BF16),
        ),
        in_specs=[vmem_spec] * 4 + [hbm_spec] * 3,
        out_specs=(vmem_spec,) * 5,
        scratch_shapes=[
            pltpu.VMEM((16, half + LANES), BF16),
            pltpu.VMEM((RING, -(-zs // 16) * 16, LANES), BF16),
            pltpu.VMEM((zs, 16, half + LANES), BF16),
            pltpu.VMEM((RING, toks, LANES), F32),
            pltpu.VMEM((toks, SLOTS), BF16),
            pltpu.VMEM((RING, SLOTS, LANES), F32),
            pltpu.VMEM((2, 2, RING, SLOTS, half), BF16),
            pltpu.VMEM((colw, 2 * LANES), BF16),
            pltpu.VMEM((LANES, colw), BF16),
            pltpu.VMEM((RING, SLOTS, 3 * LANES), F32),
            pltpu.VMEM((3, SLOTS, 3 * LANES), F32),
            pltpu.VMEM((RING, SLOTS, 3 * LANES), BF16),
            pltpu.VMEM((RING, SLOTS, half), BF16),
            pltpu.VMEM((RING, SLOTS, half), BF16),
            pltpu.VMEM((RING, SLOTS, half), F32),
            pltpu.VMEM((RING, SLOTS, half), BF16),
            pltpu.VMEM((3, SLOTS, half), BF16),
            pltpu.VMEM((8, SLOTS), F32),
            pltpu.VMEM((2 * RING, 8, SLOTS), F32),
            pltpu.VMEM((zs, 16, wide), F32),
            pltpu.VMEM((zs, 16, wide), BF16),
            pltpu.VMEM((zs - len(stops), 16, wide), BF16),
            pltpu.VMEM((len(stops) - 1, 16, wide), BF16),
            pltpu.VMEM((16, wide), BF16),
            pltpu.SemaphoreType.DMA((112 + 2 * zs,)),
            pltpu.SemaphoreType.DMA((112 + 2 * zs,)),
            pltpu.SemaphoreType.DMA((3,)),
        ],
        compiler_params=pltpu.CompilerParams(
            collective_id=0, has_side_effects=True, vmem_limit_bytes=52 * 1024 * 1024
        ),
    )(tokens, out_grad, picks, gates, w_gate, w_up, w_down)
    return in_grad, gate_grad[:, 0:top], gg, gu, gd


def solution(mesh):
    placed = (
        P(("dp", "local"), None),
        P(("dp", "local"), None),
        P(("dp", "local"), None),
        P(("dp", "local"), None),
        P("dp", None, "node"),
        P("dp", None, "node"),
        P("dp", "node", None),
    )
    return jax.shard_map(
        body,
        mesh=mesh,
        in_specs=placed,
        out_specs=(
            P(("dp", "local"), "node"),
            P(("dp", "local"), None),
            P("dp", "local", "node"),
            P("dp", "local", "node"),
            P("dp", "node", "local"),
        ),
        check_vma=False,
    )
```

```python
import functools

import jax
import jax.numpy as jnp
from jax import lax
from jax.experimental import pallas as pl
from jax.experimental.pallas import tpu as pltpu
from jax.sharding import PartitionSpec as P

F32 = jnp.float32
BF16 = jnp.bfloat16
MESH = pl.DeviceIdType.MESH
SLOTS = 128
RING = 4
LANES = 128
FIRST, MIDDLE, LATE = (0, 64), (64, 96), (96, 128)
EARLY = (0, 96)


HOP = 5


def plan(zs):
    far, near = zs // 2, -(zs - 1 - zs // 2)
    stops = [0]
    for j in range(1, far // HOP + 1):
        stops += [d for d in (HOP * j, -HOP * j) if near <= d <= far]
    seen = set(stops)
    serves = {}
    for stop in stops:
        serves[stop] = []
        for step in range(1, HOP // 2 + 1):
            for off in (step, -step):
                d = stop + off
                if near <= d <= far and d not in seen:
                    seen.add(d)
                    serves[stop].append(off)
    assert len(seen) == zs
    return stops, serves


def dot(left, right, contract=(1, 0)):
    dims = (((contract[0],), (contract[1],)), ((), ()))
    return lax.dot_general(left, right, dims, preferred_element_type=F32)


def kernel(
    sizes,
    tok_ref,
    dy_ref,
    picks_ref,
    gates_ref,
    wg_hbm,
    wu_hbm,
    wd_hbm,
    in_grad_ref,
    gate_grad_ref,
    gg_ref,
    gu_ref,
    gd_ref,
    own_chunk,
    got_chunk,
    own_meta,
    got_meta,
    ring,
    meta_tok,
    sel_tok,
    gate_slot,
    xd,
    wgu,
    wdn,
    part,
    part_in,
    hid,
    half_out,
    half_in,
    acc,
    acc_out,
    acc_in,
    gate_rows,
    dense,
    dense_out,
    near_in,
    far_in,
    last_out,
    last_in,
    send_sem,
    recv_sem,
    local_sem,
):
    zs, top = sizes
    toks = 8 * zs
    half = own_chunk.shape[1]
    colw = 2 * half
    z = lax.axis_index("dp")
    n = lax.axis_index("node")
    x = lax.axis_index("local")
    y = n // 2
    c = n % 2
    stops, serves = plan(zs)
    n_first, n_early = zs // 2, 3 * zs // 4
    order = sorted(range(zs // 2 + 1 - zs, zs // 2 + 1), key=lambda d: (abs(d), -d))
    at = order.index

    offsets = sorted({off for stop in stops for off in serves[stop]} | {HOP, -HOP})
    xr, xl, xo = (x + 1) % RING, (x + 3) % RING, (x + 2) % RING
    yr, yl, yo = (y + 1) % RING, (y + 3) % RING, (y + 2) % RING
    nodes = 2 * RING
    sibling = (z, 2 * y + 1 - c, x)
    y_right, y_left = (z, 2 * yr + c, x), (z, 2 * yl + c, x)
    x_right, x_left, x_over = (z, n, xr), (z, n, xl), (z, n, xo)
    y_over = (z, 2 * yo + c, x)
    across = (z, 2 * x + c, y)
    moved = x != y

    count = [0]
    sends = []

    def remote(src, dst, device, keep=True):
        i = count[0]
        count[0] += 1
        copy = pltpu.make_async_remote_copy(
            src_ref=src,
            dst_ref=dst,
            send_sem=send_sem.at[i],
            recv_sem=recv_sem.at[i],
            device_id=device,
            device_id_type=MESH,
        )
        if keep:
            sends.append(copy)
        return copy

    row0 = pl.multiple_of(x * colw, LANES)
    loads = [
        pltpu.make_async_copy(
            wg_hbm.at[0, pl.ds(row0, colw), :], wgu.at[:, 0:LANES], local_sem.at[0]
        ),
        pltpu.make_async_copy(
            wu_hbm.at[0, pl.ds(row0, colw), :], wgu.at[:, LANES : 2 * LANES], local_sem.at[1]
        ),
        pltpu.make_async_copy(wd_hbm.at[0, :, pl.ds(row0, colw)], wdn, local_sem.at[2]),
    ]
    for load in loads:
        load.start()

    barrier = pltpu.get_barrier_semaphore()
    peers = [((z + off + zs) % zs, n, x) for off in offsets]
    peers += [(z, n, (x + i) % RING) for i in range(1, RING)]
    peers += [(z, (n + i) % nodes, x) for i in range(1, nodes)]
    for peer in peers:
        pl.semaphore_signal(barrier, inc=1, device_id=peer, device_id_type=MESH)

    @pl.when(moved)
    def _():
        pl.semaphore_signal(barrier, inc=1, device_id=across, device_id_type=MESH)

    col0 = pl.multiple_of(y * colw + c * half, LANES)
    own_chunk[...] = jnp.concatenate(
        [tok_ref[:, pl.ds(col0, half)].astype(F32), dy_ref[:, pl.ds(col0, half)].astype(F32)],
        axis=0,
    ).astype(BF16)
    place = lax.broadcasted_iota(jnp.int32, (top, LANES), 0)
    lane_k = lax.broadcasted_iota(jnp.int32, (top, LANES), 1)
    put_picks = (lane_k == 32 * x + place).astype(F32).astype(BF16)
    put_gates = (lane_k == 32 * x + 8 + place).astype(F32).astype(BF16)
    meta = dot(picks_ref[...].astype(F32).astype(BF16), put_picks) + dot(gates_ref[...], put_gates)
    own_meta[...] = jnp.concatenate([meta, meta], axis=0).astype(BF16)
    got_meta[x] = own_meta[...]

    pl.semaphore_wait(barrier, len(peers) + jnp.where(moved, 1, 0))

    cross = remote(own_chunk, got_chunk, across, keep=False)

    @pl.when(moved)
    def _():
        cross.start()

    @pl.when(jnp.logical_not(moved))
    def _():
        got_chunk[...] = own_chunk[...]

    metas = [
        remote(own_meta, got_meta.at[x], (z, n, (x + i) % RING)) for i in range(1, RING)
    ]
    for copy in metas:
        copy.start()
    for copy in metas:
        copy.wait_recv()
    ring[at(0), :, half:] = (
        (got_meta[0].astype(F32) + got_meta[1].astype(F32))
        + (got_meta[2].astype(F32) + got_meta[3].astype(F32))
    ).astype(BF16)

    @pl.when(moved)
    def _():
        cross.wait_recv()

    ring[at(0), :, 0:half] = got_chunk[...]

    coming = {}

    def pass_on(d, off):
        copy = remote(ring.at[at(d)], ring.at[at(d + off)], ((z + off + zs) % zs, n, x))
        copy.start()
        coming[d + off] = copy

    def serve(stop):
        if stop != 0:
            coming[stop].wait_recv()
        for step in (HOP, -HOP):
            if stop * step >= 0 and stop + step in stops:
                pass_on(stop, step)
        for off in serves[stop]:
            pass_on(stop, off)

    soon = [stop for stop in stops if abs(stop) <= zs // 4 + HOP // 2]
    for stop in soon:
        serve(stop)

    expert = z.astype(F32)

    def counts(shape, axis):
        return lax.broadcasted_iota(jnp.int32, shape, axis)

    def named(metas, group):
        lane = counts(metas.shape, 1)
        near = jnp.logical_and(lane >= 32 * group, lane < 32 * group + top)
        return jnp.logical_and(metas == expert, near)

    def select(metas, group, first):
        tall = metas.shape[0]
        t_row, t_col = counts((tall, tall), 0), counts((tall, tall), 1)
        before = jnp.logical_and(t_row // 8 == t_col // 8, t_col < t_row).astype(F32).astype(BF16)
        lane = counts(metas.shape, 1)
        chunk = first + counts(metas.shape, 0) // 8
        home = jnp.where(chunk < n_first, chunk, chunk - n_first + MIDDLE[0] // 4)
        home = jnp.where(chunk < n_early, home, chunk - n_early + LATE[0] // 4)
        chosen = jnp.sum(named(metas, group).astype(F32), axis=1, keepdims=True)
        chosen = jnp.broadcast_to(chosen, metas.shape)
        rank = dot(before, chosen.astype(BF16))
        ok = jnp.logical_and(chosen > 0.5, rank == (lane % 4).astype(F32))
        return jnp.logical_and(ok, home == lane // 4).astype(F32)

    def pieces(batch):
        rows = slice(*batch)

        def move(p, group, device):
            ref = xd.at[c, p, group, rows]
            return remote(ref, ref, device)

        copies = dict(
            right=[move(p, y, y_right) for p in range(2)],
            left=[move(p, y, y_left) for p in range(2)],
            core=[move(p, y, sibling) for p in range(2)],
            core_l=[move(p, yl, sibling) for p in range(2)],
            core_r=[move(p, yr, sibling) for p in range(2)],
            core_o=[move(p, yo, sibling) for p in range(2)],
        )
        if batch == LATE:
            copies["over"] = [move(p, y, y_over) for p in range(2)]
        else:
            copies["on_right"] = move(0, yl, y_right)
            copies["on_left"] = move(1, yr, y_left)
        return copies

    def send_picked(batch, first, last):
        number = last - first
        for d in order:
            if d not in stops and first <= at(d) < last:
                coming[d].wait_recv()
        metas = ring[first:last, :, half:].astype(F32)[:, 0:8, :].reshape(8 * number, LANES)
        meta_tok[8 * first : 8 * last] = metas
        cube = select(metas, y, first).reshape(number, 8, SLOTS)
        blank = jnp.zeros_like(cube)
        pick_rows = jnp.concatenate(
            [jnp.concatenate([cube, blank], axis=2), jnp.concatenate([blank, cube], axis=2)],
            axis=1,
        ).reshape(16 * number, 2 * SLOTS)
        chunks = ring[first:last, :, 0:half].reshape(16 * number, half)
        picked = dot(pick_rows.astype(BF16), chunks, (0, 0)).astype(BF16)
        lo, hi = batch
        xd[c, 0, y, lo:hi] = picked[lo:hi]
        xd[c, 1, y, lo:hi] = picked[SLOTS + lo : SLOTS + hi]
        copies = pieces(batch)
        for copy in copies.get("over", []):
            copy.start()
        copies["right"][0].start()
        copies["left"][1].start()
        copies["right"][1].start()
        copies["left"][0].start()
        copies["core"][0].start()
        copies["core"][1].start()
        return copies

    def relay_picked(copies):
        for p in range(2):
            copies["right"][p].wait_recv()
            if p == 0 and "on_right" in copies:
                copies["on_right"].start()
            copies["core_l"][p].start()
            copies["left"][1 - p].wait_recv()
            if p == 0 and "on_left" in copies:
                copies["on_left"].start()
            copies["core_r"][1 - p].start()

    def finish_picked(copies):
        far = copies["over"] if "over" in copies else [copies["on_right"], copies["on_left"]]
        for p in range(2):
            far[p].wait_recv()
            copies["core_o"][p].start()

    def end_picked(copies):
        for name in ("core", "core_l", "core_r", "core_o"):
            for copy in copies[name]:
                copy.wait_recv()

    early = send_picked(FIRST, 0, n_first)
    for stop in stops[len(soon) :]:
        serve(stop)
    middle = send_picked(MIDDLE, n_first, n_early)
    late = send_picked(LATE, n_early, zs)

    meta_all = meta_tok[...]
    rolled = pltpu.roll(meta_all, LANES - 8, 1)
    for group in range(RING):
        chosen = select(meta_all, group, 0).astype(BF16)
        sel_tok[group] = chosen
        gate_of = jnp.sum(jnp.where(named(meta_all, group), rolled, 0.0), axis=1, keepdims=True)
        gate_of = jnp.broadcast_to(gate_of, (toks, LANES)).astype(BF16)
        gate_slot[group] = dot(chosen, gate_of, (0, 0))

    for load in loads:
        load.wait()
    relay_picked(early)
    relay_picked(middle)
    relay_picked(late)
    finish_picked(early)
    finish_picked(middle)
    end_picked(early)
    end_picked(middle)

    n_slots = RING * SLOTS

    def halves(batch):
        first, last = batch
        middle = (first + last) // 2
        return slice(first, middle), slice(middle, last)

    def scatter_copies(batch, src, into, r, l, o, right, left, over):
        if batch == LATE:
            rows = slice(*batch)
            return dict(
                far=remote(src.at[o, rows], into.at[0, rows], over),
                right=remote(src.at[r, rows], into.at[1, rows], right),
                left=remote(src.at[l, rows], into.at[2, rows], left),
            )
        lo, hi = halves(batch)
        return dict(
            a1=remote(src.at[o, lo], into.at[0, lo], right),
            b1=remote(src.at[o, hi], into.at[0, hi], left),
            a2=remote(src.at[r, hi], into.at[1, hi], right),
            b2=remote(src.at[l, lo], into.at[2, lo], left),
            a3=remote(src.at[r, lo], into.at[1, lo], right),
            b3=remote(src.at[l, hi], into.at[2, hi], left),
        )

    def send_partial(batch):
        first, last = batch
        tall = RING * (last - first)

        def take(side, p):
            return xd[side, p, :, first:last, :].reshape(tall, half)

        gate_up = dot(take(0, 0), wgu[0:half]) + dot(take(1, 0), wgu[half:])
        back_part = dot(take(0, 1), wdn[:, 0:half], (1, 1)) + dot(
            take(1, 1), wdn[:, half:], (1, 1)
        )
        part[:, first:last, 0:256] = gate_up.reshape(RING, last - first, 256)
        part[:, first:last, 256:] = back_part.reshape(RING, last - first, LANES)
        copies = scatter_copies(batch, part, part_in, xr, xl, xo, x_right, x_left, x_over)
        for name in ("far", "right", "left") if batch == LATE else ("a1", "b1", "a2", "b2"):
            copies[name].start()
        return copies

    def relay_partial(copies, batch):
        lo, hi = halves(batch)
        copies["a1"].wait_recv()
        part[xr, lo] = part[xr, lo] + part_in[0, lo]
        copies["a3"].start()
        copies["b1"].wait_recv()
        part[xl, hi] = part[xl, hi] + part_in[0, hi]
        copies["b3"].start()

    def send_hidden(copies, batch):
        rows = slice(*batch)
        for name in ("far", "right", "left") if batch == LATE else ("a2", "b2", "a3", "b3"):
            copies[name].wait_recv()
        summed = part[x, rows] + part_in[1, rows] + part_in[2, rows]
        if batch == LATE:
            summed = summed + part_in[0, rows]
        gate_pre = summed[:, 0:128]
        up_pre = summed[:, 128:256]
        back = summed[:, 256:384]
        gate_col = gate_slot[x, rows]
        sig = jax.nn.sigmoid(gate_pre)
        act = gate_pre * sig * up_pre
        d_act = gate_col * back
        d_up = d_act * gate_pre * sig
        d_pre = d_act * up_pre * sig * (1.0 + gate_pre * (1.0 - sig))
        hid[x, rows, 0:128] = d_pre.astype(BF16)
        hid[x, rows, 128:256] = d_up.astype(BF16)
        hid[x, rows, 256:384] = act.astype(BF16)
        mine = hid.at[x, rows]
        moves = [remote(mine, mine, x_right), remote(mine, mine, x_left)]
        if batch == LATE:
            moves.append(remote(mine, mine, x_over))
        for move in moves:
            move.start()
        if batch != LATE:
            lo, hi = halves(batch)
            moves.append(remote(hid.at[xl, lo], hid.at[xl, lo], x_right))
            moves.append(remote(hid.at[xr, hi], hid.at[xr, hi], x_left))
        return moves, back * act

    def relay_hidden(moves):
        moves[0].wait_recv()
        moves[2].start()
        moves[1].wait_recv()
        moves[3].start()

    px_early = send_partial(EARLY)
    finish_picked(late)
    relay_partial(px_early, EARLY)
    end_picked(late)
    px_late = send_partial(LATE)
    h_early, gates_early = send_hidden(px_early, EARLY)
    relay_hidden(h_early)
    h_late, gates_late = send_hidden(px_late, LATE)

    gate_parts = jnp.concatenate([gates_early, gates_late], axis=0)
    gate_row = jnp.sum(jnp.transpose(gate_parts), axis=0, keepdims=True)
    gate_rows[n] = jnp.broadcast_to(gate_row, (8, SLOTS))
    rows_out = [
        remote(gate_rows.at[n], gate_rows.at[n], (z, (n + i) % nodes, x)) for i in range(1, nodes)
    ]
    for copy in rows_out:
        copy.start()

    for copy in h_early[2:] + h_late:
        copy.wait_recv()

    grads = hid[:, :, 0:256].reshape(n_slots, 256)
    other = pl.multiple_of((1 - c) * half, LANES)
    ours = pl.multiple_of(c * half, LANES)
    half_out[...] = (
        dot(grads, wgu[pl.ds(other, half), :], (1, 1)).astype(BF16).reshape(RING, SLOTS, half)
    )
    core_half = {}
    for batch in (LATE, EARLY):
        rows = slice(*batch)
        core_half[batch] = remote(half_out.at[:, rows], half_in.at[:, rows], sibling)
        core_half[batch].start()
    acc[...] = dot(grads, wgu[pl.ds(ours, half), :], (1, 1)).reshape(RING, SLOTS, half)

    py = {}
    for batch in (LATE, EARLY):
        rows = slice(*batch)
        lo, hi = halves(batch)
        core_half[batch].wait_recv()
        acc[:, rows] = acc[:, rows] + half_in[:, rows].astype(F32)
        py[batch] = scatter_copies(batch, acc_out, acc_in, yr, yl, yo, y_right, y_left, y_over)
        acc_out[yo, rows] = acc[yo, rows].astype(BF16)
        if batch == LATE:
            py[batch]["far"].start()
            acc_out[yr, rows] = acc[yr, rows].astype(BF16)
            py[batch]["right"].start()
            acc_out[yl, rows] = acc[yl, rows].astype(BF16)
            py[batch]["left"].start()
        else:
            py[batch]["a1"].start()
            py[batch]["b1"].start()
            acc_out[yr, hi] = acc[yr, hi].astype(BF16)
            py[batch]["a2"].start()
            acc_out[yl, lo] = acc[yl, lo].astype(BF16)
            py[batch]["b2"].start()

    for copy in rows_out:
        copy.wait_recv()
    gate_sum = gate_rows[0]
    for i in range(1, nodes):
        gate_sum = gate_sum + gate_rows[i]
    gate_tok = jnp.sum(sel_tok[x].astype(F32) * gate_sum[0:1], axis=1, keepdims=True)
    meta_x = jnp.zeros((toks, LANES), F32)
    for i in range(RING):
        turned = meta_tok[...] if i == 0 else pltpu.roll(meta_tok[...], LANES - 32 * i, 1)
        meta_x = jnp.where(x == i, turned, meta_x)
    hit = jnp.logical_and(meta_x == expert, counts((toks, LANES), 1) < top)
    gate_hi = gate_tok.astype(BF16).astype(F32)
    gate_tile = jnp.where(hit, gate_hi, 0.0) + pltpu.roll(
        jnp.where(hit, gate_tok - gate_hi, 0.0), LANES // 2, 1
    )

    def relay_sums(batch):
        lo, hi = halves(batch)
        py[batch]["a1"].wait_recv()
        acc_out[yr, lo] = (acc[yr, lo] + acc_in[0, lo].astype(F32)).astype(BF16)
        py[batch]["a3"].start()
        py[batch]["b1"].wait_recv()
        acc_out[yl, hi] = (acc[yl, hi] + acc_in[0, hi].astype(F32)).astype(BF16)
        py[batch]["b3"].start()

    wide = (half + LANES) // 2

    def spread_sums(batch, first, last):
        rows = slice(*batch)
        for name in ("far", "right", "left") if batch == LATE else ("a2", "b2", "a3", "b3"):
            py[batch][name].wait_recv()
        total = acc[y, rows] + acc_in[1, rows].astype(F32) + acc_in[2, rows].astype(F32)
        if batch == LATE:
            total = total + acc_in[0, rows].astype(F32)
        blank = jnp.zeros((SLOTS - (batch[1] - batch[0]), half), F32)
        total = jnp.concatenate([total, blank] if batch == EARLY else [blank, total], axis=0)
        sel = sel_tok[y, 8 * first : 8 * last]
        one = total.astype(BF16)
        rest = total - one.astype(F32)
        two = rest.astype(BF16)
        three = (rest - two.astype(F32)).astype(BF16)
        spread = dot(sel, one) + (dot(sel, two) + dot(sel, three))
        full = jnp.concatenate([spread, gate_tile[8 * first : 8 * last]], axis=1)
        dense[first:last, 0:8, :] = full[:, 0:wide].reshape(last - first, 8, wide)
        dense[first:last, 8:16, :] = full[:, wide:].reshape(last - first, 8, wide)
        dense_out[first:last] = dense[first:last].astype(BF16)

    near = {}

    def send_near(first, last):
        for stop in reversed(stops):
            for off in serves[stop]:
                if first <= at(stop + off) < last:
                    near[stop, off] = remote(
                        dense_out.at[at(stop + off)],
                        near_in.at[len(near)],
                        ((z - off + zs) % zs, n, x),
                    )
                    near[stop, off].start()

    spread_sums(LATE, n_early, zs)
    send_near(n_early, zs)
    relay_sums(EARLY)
    spread_sums(EARLY, 0, n_early)
    send_near(0, n_early)
    slot_of = {key: i for i, key in enumerate(near)}

    tiles = colw // LANES
    def weight_tile(t):
        side = t // (half // LANES)
        left = pl.multiple_of((t % (half // LANES)) * LANES, LANES)
        down = pl.multiple_of(t * LANES, LANES)
        xs = xd[side, 0, :, :, pl.ds(left, LANES)].reshape(n_slots, LANES)
        ds = xd[side, 1, :, :, pl.ds(left, LANES)].astype(F32)
        scaled = (gate_slot[...] * ds).astype(BF16).reshape(n_slots, LANES)
        both = dot(xs, hid[:, :, 0:256].reshape(n_slots, 256), (0, 0)).astype(BF16)
        gg_ref[0, pl.ds(down, LANES), :] = both[:, 0:128]
        gu_ref[0, pl.ds(down, LANES), :] = both[:, 128:256]
        gd_ref[0, :, pl.ds(down, LANES)] = dot(
            hid[:, :, 256:384].reshape(n_slots, LANES), scaled, (0, 0)
        ).astype(BF16)

    def weight_tiles(first, last):
        def one(t, carry):
            weight_tile(t)
            return carry

        lax.fori_loop(first, last, one, 0)

    levels = len(stops) // 2
    share = -(-tiles // (levels + 1))
    weight_tiles(0, min(share, tiles))
    far = {}
    for i, stop in enumerate(reversed(stops)):
        value = dense[at(stop)]
        for off in serves[stop]:
            near[stop, off].wait_recv()
            value = value + near_in[slot_of[stop, off]].astype(F32)
        for step in (HOP, -HOP):
            if stop * step >= 0 and stop + step in stops:
                far[stop + step].wait_recv()
                value = value + far_in[stops.index(stop + step) - 1].astype(F32)
        if stop == 0:
            final = value
        else:
            dense_out[at(stop)] = value.astype(BF16)
            back_by = HOP if stop > 0 else -HOP
            far[stop] = remote(
                dense_out.at[at(stop)],
                far_in.at[stops.index(stop) - 1],
                ((z - back_by + zs) % zs, n, x),
            )
            far[stop].start()
            if i % 2 == 1:
                done = share * ((i + 1) // 2)
                weight_tiles(min(done, tiles), min(done + share, tiles))
    final = jnp.concatenate([final[0:8], final[8:16]], axis=1)
    gate_both = final[:, half:]
    gate_grad_ref[...] = gate_both + pltpu.roll(gate_both, LANES // 2, 1)
    last_out[...] = final[:, 0:half]
    end = remote(last_out, last_in, across, keep=False)

    @pl.when(moved)
    def _():
        end.start()
        end.wait_recv()

    @pl.when(jnp.logical_not(moved))
    def _():
        last_in[...] = last_out[...]

    in_grad_ref[...] = last_in[...].astype(BF16)

    @pl.when(moved)
    def _():
        cross.wait_send()
        end.wait_send()

    for copy in sends:
        copy.wait_send()


def body(tokens, out_grad, picks, gates, w_gate, w_up, w_down):
    zs = lax.axis_size("dp")
    width = tokens.shape[1]
    top = picks.shape[1]
    half = width // (2 * RING)
    colw = 2 * half
    toks = 8 * zs
    wide = (half + LANES) // 2
    stops, _ = plan(zs)
    hbm_spec = pl.BlockSpec(memory_space=pltpu.HBM)
    vmem_spec = pl.BlockSpec(memory_space=pltpu.VMEM)
    in_grad, gate_grad, gg, gu, gd = pl.pallas_call(
        functools.partial(kernel, (zs, top)),
        out_shape=(
            jax.ShapeDtypeStruct((8, half), BF16),
            jax.ShapeDtypeStruct((8, LANES), F32),
            jax.ShapeDtypeStruct((1, colw, LANES), BF16),
            jax.ShapeDtypeStruct((1, colw, LANES), BF16),
            jax.ShapeDtypeStruct((1, LANES, colw), BF16),
        ),
        in_specs=[vmem_spec] * 4 + [hbm_spec] * 3,
        out_specs=(vmem_spec,) * 5,
        scratch_shapes=[
            pltpu.VMEM((16, half), BF16),
            pltpu.VMEM((16, half), BF16),
            pltpu.VMEM((16, LANES), BF16),
            pltpu.VMEM((RING, 16, LANES), BF16),
            pltpu.VMEM((zs, 16, half + LANES), BF16),
            pltpu.VMEM((toks, LANES), F32),
            pltpu.VMEM((RING, toks, SLOTS), BF16),
            pltpu.VMEM((RING, SLOTS, LANES), F32),
            pltpu.VMEM((2, 2, RING, SLOTS, half), BF16),
            pltpu.VMEM((colw, 2 * LANES), BF16),
            pltpu.VMEM((LANES, colw), BF16),
            pltpu.VMEM((RING, SLOTS, 3 * LANES), F32),
            pltpu.VMEM((3, SLOTS, 3 * LANES), F32),
            pltpu.VMEM((RING, SLOTS, 3 * LANES), BF16),
            pltpu.VMEM((RING, SLOTS, half), BF16),
            pltpu.VMEM((RING, SLOTS, half), BF16),
            pltpu.VMEM((RING, SLOTS, half), F32),
            pltpu.VMEM((RING, SLOTS, half), BF16),
            pltpu.VMEM((3, SLOTS, half), BF16),
            pltpu.VMEM((2 * RING, 8, SLOTS), F32),
            pltpu.VMEM((zs, 16, wide), F32),
            pltpu.VMEM((zs, 16, wide), BF16),
            pltpu.VMEM((zs - len(stops), 16, wide), BF16),
            pltpu.VMEM((len(stops) - 1, 16, wide), BF16),
            pltpu.VMEM((8, half), F32),
            pltpu.VMEM((8, half), F32),
            pltpu.SemaphoreType.DMA((112 + 2 * zs,)),
            pltpu.SemaphoreType.DMA((112 + 2 * zs,)),
            pltpu.SemaphoreType.DMA((3,)),
        ],
        compiler_params=pltpu.CompilerParams(
            collective_id=0, has_side_effects=True, vmem_limit_bytes=52 * 1024 * 1024
        ),
    )(tokens, out_grad, picks, gates, w_gate, w_up, w_down)
    return in_grad, gate_grad[:, 0:top], gg, gu, gd


def solution(mesh):
    placed = (
        P(("dp", "local"), None),
        P(("dp", "local"), None),
        P(("dp", "local"), None),
        P(("dp", "local"), None),
        P("dp", None, "node"),
        P("dp", None, "node"),
        P("dp", "node", None),
    )
    return jax.shard_map(
        body,
        mesh=mesh,
        in_specs=placed,
        out_specs=(
            P(("dp", "local"), "node"),
            P(("dp", "local"), None),
            P("dp", "local", "node"),
            P("dp", "local", "node"),
            P("dp", "node", "local"),
        ),
        check_vma=False,
    )
```

```python
import functools

import jax
import jax.numpy as jnp
from jax import lax
from jax.experimental import pallas as pl
from jax.experimental.pallas import tpu as pltpu
from jax.sharding import PartitionSpec as P

F32 = jnp.float32
BF16 = jnp.bfloat16
MESH = pl.DeviceIdType.MESH
SLOTS = 128
RING = 4
LANES = 128
FIRST, MIDDLE, LATE = (0, 64), (64, 96), (96, 128)
EARLY = (0, 96)


HOP = 5


def plan(zs):
    far, near = zs // 2, -(zs - 1 - zs // 2)
    stops = [0]
    for j in range(1, far // HOP + 1):
        stops += [d for d in (HOP * j, -HOP * j) if near <= d <= far]
    seen = set(stops)
    serves = {}
    for stop in stops:
        serves[stop] = []
        for step in range(1, HOP // 2 + 1):
            for off in (step, -step):
                d = stop + off
                if near <= d <= far and d not in seen:
                    seen.add(d)
                    serves[stop].append(off)
    assert len(seen) == zs
    return stops, serves


def dot(left, right, contract=(1, 0)):
    dims = (((contract[0],), (contract[1],)), ((), ()))
    return lax.dot_general(left, right, dims, preferred_element_type=F32)


def kernel(
    sizes,
    tok_ref,
    dy_ref,
    picks_ref,
    gates_ref,
    wg_hbm,
    wu_hbm,
    wd_hbm,
    in_grad_ref,
    gate_grad_ref,
    gg_ref,
    gu_ref,
    gd_ref,
    own_chunk,
    got_chunk,
    own_meta,
    got_meta,
    ring,
    meta_tok,
    sel_tok,
    gate_slot,
    xd,
    wgu,
    wdn,
    part,
    part_in,
    hid,
    half_out,
    half_in,
    acc,
    acc_out,
    acc_in,
    gate_rows,
    dense,
    dense_out,
    near_in,
    far_in,
    last_out,
    last_in,
    send_sem,
    recv_sem,
    local_sem,
):
    zs, top = sizes
    toks = 8 * zs
    half = own_chunk.shape[1]
    colw = 2 * half
    z = lax.axis_index("dp")
    n = lax.axis_index("node")
    x = lax.axis_index("local")
    y = n // 2
    c = n % 2
    stops, serves = plan(zs)
    n_first, n_early = zs // 2, 3 * zs // 4
    order = sorted(range(zs // 2 + 1 - zs, zs // 2 + 1), key=lambda d: (abs(d), -d))
    at = order.index

    offsets = sorted({off for stop in stops for off in serves[stop]} | {HOP, -HOP})
    xr, xl, xo = (x + 1) % RING, (x + 3) % RING, (x + 2) % RING
    yr, yl, yo = (y + 1) % RING, (y + 3) % RING, (y + 2) % RING
    nodes = 2 * RING
    sibling = (z, 2 * y + 1 - c, x)
    y_right, y_left = (z, 2 * yr + c, x), (z, 2 * yl + c, x)
    x_right, x_left, x_over = (z, n, xr), (z, n, xl), (z, n, xo)
    y_over = (z, 2 * yo + c, x)
    across = (z, 2 * x + c, y)
    moved = x != y

    count = [0]
    sends = []

    def remote(src, dst, device, keep=True):
        i = count[0]
        count[0] += 1
        copy = pltpu.make_async_remote_copy(
            src_ref=src,
            dst_ref=dst,
            send_sem=send_sem.at[i],
            recv_sem=recv_sem.at[i],
            device_id=device,
            device_id_type=MESH,
        )
        if keep:
            sends.append(copy)
        return copy

    row0 = pl.multiple_of(x * colw, LANES)
    loads = [
        pltpu.make_async_copy(
            wg_hbm.at[0, pl.ds(row0, colw), :], wgu.at[:, 0:LANES], local_sem.at[0]
        ),
        pltpu.make_async_copy(
            wu_hbm.at[0, pl.ds(row0, colw), :], wgu.at[:, LANES : 2 * LANES], local_sem.at[1]
        ),
        pltpu.make_async_copy(wd_hbm.at[0, :, pl.ds(row0, colw)], wdn, local_sem.at[2]),
    ]
    for load in loads:
        load.start()

    barrier = pltpu.get_barrier_semaphore()
    peers = [((z + off + zs) % zs, n, x) for off in offsets]
    peers += [(z, n, (x + i) % RING) for i in range(1, RING)]
    peers += [(z, (n + i) % nodes, x) for i in range(1, nodes)]
    for peer in peers:
        pl.semaphore_signal(barrier, inc=1, device_id=peer, device_id_type=MESH)

    @pl.when(moved)
    def _():
        pl.semaphore_signal(barrier, inc=1, device_id=across, device_id_type=MESH)

    col0 = pl.multiple_of(y * colw + c * half, LANES)
    own_chunk[...] = jnp.concatenate(
        [tok_ref[:, pl.ds(col0, half)].astype(F32), dy_ref[:, pl.ds(col0, half)].astype(F32)],
        axis=0,
    ).astype(BF16)
    place = lax.broadcasted_iota(jnp.int32, (top, LANES), 0)
    lane_k = lax.broadcasted_iota(jnp.int32, (top, LANES), 1)
    put_picks = (lane_k == 32 * x + place).astype(F32).astype(BF16)
    put_gates = (lane_k == 32 * x + 8 + place).astype(F32).astype(BF16)
    meta = dot(picks_ref[...].astype(F32).astype(BF16), put_picks) + dot(gates_ref[...], put_gates)
    own_meta[...] = jnp.concatenate([meta, meta], axis=0).astype(BF16)
    got_meta[x] = own_meta[...]

    pl.semaphore_wait(barrier, len(peers) + jnp.where(moved, 1, 0))

    cross = remote(own_chunk, got_chunk, across, keep=False)

    @pl.when(moved)
    def _():
        cross.start()

    @pl.when(jnp.logical_not(moved))
    def _():
        got_chunk[...] = own_chunk[...]

    metas = [
        remote(own_meta, got_meta.at[x], (z, n, (x + i) % RING)) for i in range(1, RING)
    ]
    for copy in metas:
        copy.start()
    for copy in metas:
        copy.wait_recv()
    ring[at(0), :, half:] = (
        (got_meta[0].astype(F32) + got_meta[1].astype(F32))
        + (got_meta[2].astype(F32) + got_meta[3].astype(F32))
    ).astype(BF16)

    @pl.when(moved)
    def _():
        cross.wait_recv()

    ring[at(0), :, 0:half] = got_chunk[...]

    coming = {}

    def pass_on(d, off):
        copy = remote(ring.at[at(d)], ring.at[at(d + off)], ((z + off + zs) % zs, n, x))
        copy.start()
        coming[d + off] = copy

    def serve(stop):
        if stop != 0:
            coming[stop].wait_recv()
        for step in (HOP, -HOP):
            if stop * step >= 0 and stop + step in stops:
                pass_on(stop, step)
        for off in serves[stop]:
            pass_on(stop, off)

    soon = [stop for stop in stops if abs(stop) <= zs // 4 + HOP // 2]
    for stop in soon:
        serve(stop)

    expert = z.astype(F32)

    def counts(shape, axis):
        return lax.broadcasted_iota(jnp.int32, shape, axis)

    def named(metas, group):
        lane = counts(metas.shape, 1)
        near = jnp.logical_and(lane >= 32 * group, lane < 32 * group + top)
        return jnp.logical_and(metas == expert, near)

    def select(metas, group, first):
        tall = metas.shape[0]
        t_row, t_col = counts((tall, tall), 0), counts((tall, tall), 1)
        before = jnp.logical_and(t_row // 8 == t_col // 8, t_col < t_row).astype(F32).astype(BF16)
        lane = counts(metas.shape, 1)
        chunk = first + counts(metas.shape, 0) // 8
        home = jnp.where(chunk < n_first, chunk, chunk - n_first + MIDDLE[0] // 4)
        home = jnp.where(chunk < n_early, home, chunk - n_early + LATE[0] // 4)
        chosen = jnp.sum(named(metas, group).astype(F32), axis=1, keepdims=True)
        chosen = jnp.broadcast_to(chosen, metas.shape)
        rank = dot(before, chosen.astype(BF16))
        ok = jnp.logical_and(chosen > 0.5, rank == (lane % 4).astype(F32))
        return jnp.logical_and(ok, home == lane // 4).astype(F32)

    def pieces(batch):
        rows = slice(*batch)

        def move(p, group, device):
            ref = xd.at[c, p, group, rows]
            return remote(ref, ref, device)

        copies = dict(
            right=[move(p, y, y_right) for p in range(2)],
            left=[move(p, y, y_left) for p in range(2)],
            core=[move(p, y, sibling) for p in range(2)],
            core_l=[move(p, yl, sibling) for p in range(2)],
            core_r=[move(p, yr, sibling) for p in range(2)],
            core_o=[move(p, yo, sibling) for p in range(2)],
        )
        if batch == LATE:
            copies["over"] = [move(p, y, y_over) for p in range(2)]
        else:
            copies["on_right"] = move(0, yl, y_right)
            copies["on_left"] = move(1, yr, y_left)
        return copies

    def send_picked(batch, first, last):
        number = last - first
        for d in order:
            if d not in stops and first <= at(d) < last:
                coming[d].wait_recv()
        metas = ring[first:last, :, half:].astype(F32)[:, 0:8, :].reshape(8 * number, LANES)
        meta_tok[8 * first : 8 * last] = metas
        cube = select(metas, y, first).reshape(number, 8, SLOTS)
        blank = jnp.zeros_like(cube)
        pick_rows = jnp.concatenate(
            [jnp.concatenate([cube, blank], axis=2), jnp.concatenate([blank, cube], axis=2)],
            axis=1,
        ).reshape(16 * number, 2 * SLOTS)
        chunks = ring[first:last, :, 0:half].reshape(16 * number, half)
        picked = dot(pick_rows.astype(BF16), chunks, (0, 0)).astype(BF16)
        lo, hi = batch
        xd[c, 0, y, lo:hi] = picked[lo:hi]
        xd[c, 1, y, lo:hi] = picked[SLOTS + lo : SLOTS + hi]
        copies = pieces(batch)
        for copy in copies.get("over", []):
            copy.start()
        copies["right"][0].start()
        copies["left"][1].start()
        copies["right"][1].start()
        copies["left"][0].start()
        copies["core"][0].start()
        copies["core"][1].start()
        return copies

    def relay_picked(copies):
        for p in range(2):
            copies["right"][p].wait_recv()
            if p == 0 and "on_right" in copies:
                copies["on_right"].start()
            copies["core_l"][p].start()
            copies["left"][1 - p].wait_recv()
            if p == 0 and "on_left" in copies:
                copies["on_left"].start()
            copies["core_r"][1 - p].start()

    def finish_picked(copies):
        far = copies["over"] if "over" in copies else [copies["on_right"], copies["on_left"]]
        for p in range(2):
            far[p].wait_recv()
            copies["core_o"][p].start()

    def end_picked(copies):
        for name in ("core", "core_l", "core_r", "core_o"):
            for copy in copies[name]:
                copy.wait_recv()

    early = send_picked(FIRST, 0, n_first)
    for stop in stops[len(soon) :]:
        serve(stop)
    middle = send_picked(MIDDLE, n_first, n_early)
    late = send_picked(LATE, n_early, zs)

    meta_all = meta_tok[...]
    rolled = pltpu.roll(meta_all, LANES - 8, 1)
    for group in range(RING):
        chosen = select(meta_all, group, 0).astype(BF16)
        sel_tok[group] = chosen
        gate_of = jnp.sum(jnp.where(named(meta_all, group), rolled, 0.0), axis=1, keepdims=True)
        gate_of = jnp.broadcast_to(gate_of, (toks, LANES)).astype(BF16)
        gate_slot[group] = dot(chosen, gate_of, (0, 0))

    for load in loads:
        load.wait()
    relay_picked(early)
    relay_picked(middle)
    relay_picked(late)
    finish_picked(early)
    finish_picked(middle)
    end_picked(early)
    end_picked(middle)

    n_slots = RING * SLOTS

    def halves(batch):
        first, last = batch
        middle = (first + last) // 2
        return slice(first, middle), slice(middle, last)

    def scatter_copies(batch, src, into, r, l, o, right, left, over):
        if batch == LATE:
            rows = slice(*batch)
            return dict(
                far=remote(src.at[o, rows], into.at[0, rows], over),
                right=remote(src.at[r, rows], into.at[1, rows], right),
                left=remote(src.at[l, rows], into.at[2, rows], left),
            )
        lo, hi = halves(batch)
        return dict(
            a1=remote(src.at[o, lo], into.at[0, lo], right),
            b1=remote(src.at[o, hi], into.at[0, hi], left),
            a2=remote(src.at[r, hi], into.at[1, hi], right),
            b2=remote(src.at[l, lo], into.at[2, lo], left),
            a3=remote(src.at[r, lo], into.at[1, lo], right),
            b3=remote(src.at[l, hi], into.at[2, hi], left),
        )

    def send_partial(batch):
        first, last = batch
        tall = RING * (last - first)

        def take(side, p):
            return xd[side, p, :, first:last, :].reshape(tall, half)

        gate_up = dot(take(0, 0), wgu[0:half]) + dot(take(1, 0), wgu[half:])
        back_part = dot(take(0, 1), wdn[:, 0:half], (1, 1)) + dot(
            take(1, 1), wdn[:, half:], (1, 1)
        )
        part[:, first:last, 0:256] = gate_up.reshape(RING, last - first, 256)
        part[:, first:last, 256:] = back_part.reshape(RING, last - first, LANES)
        copies = scatter_copies(batch, part, part_in, xr, xl, xo, x_right, x_left, x_over)
        for name in ("far", "right", "left") if batch == LATE else ("a1", "b1", "a2", "b2"):
            copies[name].start()
        return copies

    def relay_partial(copies, batch):
        lo, hi = halves(batch)
        copies["a1"].wait_recv()
        part[xr, lo] = part[xr, lo] + part_in[0, lo]
        copies["a3"].start()
        copies["b1"].wait_recv()
        part[xl, hi] = part[xl, hi] + part_in[0, hi]
        copies["b3"].start()

    def send_hidden(copies, batch):
        rows = slice(*batch)
        for name in ("far", "right", "left") if batch == LATE else ("a2", "b2", "a3", "b3"):
            copies[name].wait_recv()
        summed = part[x, rows] + part_in[1, rows] + part_in[2, rows]
        if batch == LATE:
            summed = summed + part_in[0, rows]
        gate_pre = summed[:, 0:128]
        up_pre = summed[:, 128:256]
        back = summed[:, 256:384]
        gate_col = gate_slot[x, rows]
        sig = jax.nn.sigmoid(gate_pre)
        act = gate_pre * sig * up_pre
        d_act = gate_col * back
        d_up = d_act * gate_pre * sig
        d_pre = d_act * up_pre * sig * (1.0 + gate_pre * (1.0 - sig))
        hid[x, rows, 0:128] = d_pre.astype(BF16)
        hid[x, rows, 128:256] = d_up.astype(BF16)
        hid[x, rows, 256:384] = act.astype(BF16)
        mine = hid.at[x, rows]
        moves = [remote(mine, mine, x_right), remote(mine, mine, x_left)]
        if batch == LATE:
            moves.append(remote(mine, mine, x_over))
        for move in moves:
            move.start()
        if batch != LATE:
            lo, hi = halves(batch)
            moves.append(remote(hid.at[xl, lo], hid.at[xl, lo], x_right))
            moves.append(remote(hid.at[xr, hi], hid.at[xr, hi], x_left))
        return moves, back * act

    def relay_hidden(moves):
        moves[0].wait_recv()
        moves[2].start()
        moves[1].wait_recv()
        moves[3].start()

    px_early = send_partial(EARLY)
    finish_picked(late)
    relay_partial(px_early, EARLY)
    end_picked(late)
    px_late = send_partial(LATE)
    h_early, gates_early = send_hidden(px_early, EARLY)
    relay_hidden(h_early)
    h_late, gates_late = send_hidden(px_late, LATE)

    gate_parts = jnp.concatenate([gates_early, gates_late], axis=0)
    gate_row = jnp.sum(jnp.transpose(gate_parts), axis=0, keepdims=True)
    gate_rows[n] = jnp.broadcast_to(gate_row, (8, SLOTS))
    rows_out = [
        remote(gate_rows.at[n], gate_rows.at[n], (z, (n + i) % nodes, x)) for i in range(1, nodes)
    ]
    for copy in rows_out:
        copy.start()

    for copy in h_early[2:] + h_late:
        copy.wait_recv()

    grads = hid[:, :, 0:256].reshape(n_slots, 256)
    other = pl.multiple_of((1 - c) * half, LANES)
    ours = pl.multiple_of(c * half, LANES)
    half_out[...] = (
        dot(grads, wgu[pl.ds(other, half), :], (1, 1)).astype(BF16).reshape(RING, SLOTS, half)
    )
    core_half = {}
    for batch in (LATE, EARLY):
        rows = slice(*batch)
        core_half[batch] = remote(half_out.at[:, rows], half_in.at[:, rows], sibling)
        core_half[batch].start()
    acc[...] = dot(grads, wgu[pl.ds(ours, half), :], (1, 1)).reshape(RING, SLOTS, half)

    py = {}
    for batch in (LATE, EARLY):
        rows = slice(*batch)
        lo, hi = halves(batch)
        core_half[batch].wait_recv()
        acc[:, rows] = acc[:, rows] + half_in[:, rows].astype(F32)
        py[batch] = scatter_copies(batch, acc_out, acc_in, yr, yl, yo, y_right, y_left, y_over)
        acc_out[yo, rows] = acc[yo, rows].astype(BF16)
        if batch == LATE:
            py[batch]["far"].start()
            acc_out[yr, rows] = acc[yr, rows].astype(BF16)
            py[batch]["right"].start()
            acc_out[yl, rows] = acc[yl, rows].astype(BF16)
            py[batch]["left"].start()
        else:
            py[batch]["a1"].start()
            py[batch]["b1"].start()
            acc_out[yr, hi] = acc[yr, hi].astype(BF16)
            py[batch]["a2"].start()
            acc_out[yl, lo] = acc[yl, lo].astype(BF16)
            py[batch]["b2"].start()

    for copy in rows_out:
        copy.wait_recv()
    gate_sum = gate_rows[0]
    for i in range(1, nodes):
        gate_sum = gate_sum + gate_rows[i]
    gate_tok = jnp.sum(sel_tok[x].astype(F32) * gate_sum[0:1], axis=1, keepdims=True)
    meta_x = jnp.zeros((toks, LANES), F32)
    for i in range(RING):
        turned = meta_tok[...] if i == 0 else pltpu.roll(meta_tok[...], LANES - 32 * i, 1)
        meta_x = jnp.where(x == i, turned, meta_x)
    hit = jnp.logical_and(meta_x == expert, counts((toks, LANES), 1) < top)
    gate_hi = gate_tok.astype(BF16).astype(F32)
    gate_tile = jnp.where(hit, gate_hi, 0.0) + pltpu.roll(
        jnp.where(hit, gate_tok - gate_hi, 0.0), LANES // 2, 1
    )

    def relay_sums(batch):
        lo, hi = halves(batch)
        py[batch]["a1"].wait_recv()
        acc_out[yr, lo] = (acc[yr, lo] + acc_in[0, lo].astype(F32)).astype(BF16)
        py[batch]["a3"].start()
        py[batch]["b1"].wait_recv()
        acc_out[yl, hi] = (acc[yl, hi] + acc_in[0, hi].astype(F32)).astype(BF16)
        py[batch]["b3"].start()

    wide = (half + LANES) // 2

    def spread_sums(batch, first, last):
        rows = slice(*batch)
        for name in ("far", "right", "left") if batch == LATE else ("a2", "b2", "a3", "b3"):
            py[batch][name].wait_recv()
        total = acc[y, rows] + acc_in[1, rows].astype(F32) + acc_in[2, rows].astype(F32)
        if batch == LATE:
            total = total + acc_in[0, rows].astype(F32)
        blank = jnp.zeros((SLOTS - (batch[1] - batch[0]), half), F32)
        total = jnp.concatenate([total, blank] if batch == EARLY else [blank, total], axis=0)
        sel = sel_tok[y, 8 * first : 8 * last]
        one = total.astype(BF16)
        rest = total - one.astype(F32)
        two = rest.astype(BF16)
        three = (rest - two.astype(F32)).astype(BF16)
        spread = dot(sel, one) + (dot(sel, two) + dot(sel, three))
        full = jnp.concatenate([spread, gate_tile[8 * first : 8 * last]], axis=1)
        dense[first:last, 0:8, :] = full[:, 0:wide].reshape(last - first, 8, wide)
        dense[first:last, 8:16, :] = full[:, wide:].reshape(last - first, 8, wide)
        dense_out[first:last] = dense[first:last].astype(BF16)

    near = {}

    def send_near(first, last):
        for stop in reversed(stops):
            for off in serves[stop]:
                if first <= at(stop + off) < last:
                    near[stop, off] = remote(
                        dense_out.at[at(stop + off)],
                        near_in.at[len(near)],
                        ((z - off + zs) % zs, n, x),
                    )
                    near[stop, off].start()

    spread_sums(LATE, n_early, zs)
    send_near(n_early, zs)
    relay_sums(EARLY)
    spread_sums(EARLY, 0, n_early)
    send_near(0, n_early)
    slot_of = {key: i for i, key in enumerate(near)}

    tiles = colw // LANES
    def weight_tile(t):
        side = t // (half // LANES)
        left = pl.multiple_of((t % (half // LANES)) * LANES, LANES)
        down = pl.multiple_of(t * LANES, LANES)
        xs = xd[side, 0, :, :, pl.ds(left, LANES)].reshape(n_slots, LANES)
        ds = xd[side, 1, :, :, pl.ds(left, LANES)].astype(F32)
        scaled = (gate_slot[...] * ds).astype(BF16).reshape(n_slots, LANES)
        both = dot(xs, hid[:, :, 0:256].reshape(n_slots, 256), (0, 0)).astype(BF16)
        gg_ref[0, pl.ds(down, LANES), :] = both[:, 0:128]
        gu_ref[0, pl.ds(down, LANES), :] = both[:, 128:256]
        gd_ref[0, :, pl.ds(down, LANES)] = dot(
            hid[:, :, 256:384].reshape(n_slots, LANES), scaled, (0, 0)
        ).astype(BF16)

    def weight_tiles(first, last):
        def one(t, carry):
            weight_tile(t)
            return carry

        lax.fori_loop(first, last, one, 0)

    levels = len(stops) // 2
    share = -(-tiles // (levels + 1))
    lead = max(0, tiles - levels * share)
    weight_tiles(0, lead)
    far = {}
    for i, stop in enumerate(reversed(stops)):
        value = dense[at(stop)]
        for off in serves[stop]:
            near[stop, off].wait_recv()
            value = value + near_in[slot_of[stop, off]].astype(F32)
        for step in (HOP, -HOP):
            if stop * step >= 0 and stop + step in stops:
                far[stop + step].wait_recv()
                value = value + far_in[stops.index(stop + step) - 1].astype(F32)
        if stop == 0:
            final = value
        else:
            dense_out[at(stop)] = value.astype(BF16)
            back_by = HOP if stop > 0 else -HOP
            far[stop] = remote(
                dense_out.at[at(stop)],
                far_in.at[stops.index(stop) - 1],
                ((z - back_by + zs) % zs, n, x),
            )
            far[stop].start()
            if i % 2 == 1:
                done = lead + share * ((i - 1) // 2)
                weight_tiles(min(done, tiles), min(done + share, tiles))
    final = jnp.concatenate([final[0:8], final[8:16]], axis=1)
    gate_both = final[:, half:]
    gate_grad_ref[...] = gate_both + pltpu.roll(gate_both, LANES // 2, 1)
    last_out[...] = final[:, 0:half]
    end = remote(last_out, last_in, across, keep=False)

    @pl.when(moved)
    def _():
        end.start()
        end.wait_recv()

    @pl.when(jnp.logical_not(moved))
    def _():
        last_in[...] = last_out[...]

    in_grad_ref[...] = last_in[...].astype(BF16)

    @pl.when(moved)
    def _():
        cross.wait_send()
        end.wait_send()

    for copy in sends:
        copy.wait_send()


def body(tokens, out_grad, picks, gates, w_gate, w_up, w_down):
    zs = lax.axis_size("dp")
    width = tokens.shape[1]
    top = picks.shape[1]
    half = width // (2 * RING)
    colw = 2 * half
    toks = 8 * zs
    wide = (half + LANES) // 2
    stops, _ = plan(zs)
    hbm_spec = pl.BlockSpec(memory_space=pltpu.HBM)
    vmem_spec = pl.BlockSpec(memory_space=pltpu.VMEM)
    in_grad, gate_grad, gg, gu, gd = pl.pallas_call(
        functools.partial(kernel, (zs, top)),
        out_shape=(
            jax.ShapeDtypeStruct((8, half), BF16),
            jax.ShapeDtypeStruct((8, LANES), F32),
            jax.ShapeDtypeStruct((1, colw, LANES), BF16),
            jax.ShapeDtypeStruct((1, colw, LANES), BF16),
            jax.ShapeDtypeStruct((1, LANES, colw), BF16),
        ),
        in_specs=[vmem_spec] * 4 + [hbm_spec] * 3,
        out_specs=(vmem_spec,) * 5,
        scratch_shapes=[
            pltpu.VMEM((16, half), BF16),
            pltpu.VMEM((16, half), BF16),
            pltpu.VMEM((16, LANES), BF16),
            pltpu.VMEM((RING, 16, LANES), BF16),
            pltpu.VMEM((zs, 16, half + LANES), BF16),
            pltpu.VMEM((toks, LANES), F32),
            pltpu.VMEM((RING, toks, SLOTS), BF16),
            pltpu.VMEM((RING, SLOTS, LANES), F32),
            pltpu.VMEM((2, 2, RING, SLOTS, half), BF16),
            pltpu.VMEM((colw, 2 * LANES), BF16),
            pltpu.VMEM((LANES, colw), BF16),
            pltpu.VMEM((RING, SLOTS, 3 * LANES), F32),
            pltpu.VMEM((3, SLOTS, 3 * LANES), F32),
            pltpu.VMEM((RING, SLOTS, 3 * LANES), BF16),
            pltpu.VMEM((RING, SLOTS, half), BF16),
            pltpu.VMEM((RING, SLOTS, half), BF16),
            pltpu.VMEM((RING, SLOTS, half), F32),
            pltpu.VMEM((RING, SLOTS, half), BF16),
            pltpu.VMEM((3, SLOTS, half), BF16),
            pltpu.VMEM((2 * RING, 8, SLOTS), F32),
            pltpu.VMEM((zs, 16, wide), F32),
            pltpu.VMEM((zs, 16, wide), BF16),
            pltpu.VMEM((zs - len(stops), 16, wide), BF16),
            pltpu.VMEM((len(stops) - 1, 16, wide), BF16),
            pltpu.VMEM((8, half), F32),
            pltpu.VMEM((8, half), F32),
            pltpu.SemaphoreType.DMA((112 + 2 * zs,)),
            pltpu.SemaphoreType.DMA((112 + 2 * zs,)),
            pltpu.SemaphoreType.DMA((3,)),
        ],
        compiler_params=pltpu.CompilerParams(
            collective_id=0, has_side_effects=True, vmem_limit_bytes=52 * 1024 * 1024
        ),
    )(tokens, out_grad, picks, gates, w_gate, w_up, w_down)
    return in_grad, gate_grad[:, 0:top], gg, gu, gd


def solution(mesh):
    placed = (
        P(("dp", "local"), None),
        P(("dp", "local"), None),
        P(("dp", "local"), None),
        P(("dp", "local"), None),
        P("dp", None, "node"),
        P("dp", None, "node"),
        P("dp", "node", None),
    )
    return jax.shard_map(
        body,
        mesh=mesh,
        in_specs=placed,
        out_specs=(
            P(("dp", "local"), "node"),
            P(("dp", "local"), None),
            P("dp", "local", "node"),
            P("dp", "local", "node"),
            P("dp", "node", "local"),
        ),
        check_vma=False,
    )
```
